256 devices in a mesh: rep: 32 (over z, x_lo, core), shard: 8 (over x_hi, y).
Axes of the slice: x: 4 (x_hi: 2, x_lo: 2; x = x_hi * 2 + x_lo), y: 4, z: 8, core: 2. Of those that a mesh axis runs over, the one named last changes fastest.
Arguments:
- hidden_in: bfloat16 [49152, 8192], P(('rep', 'shard')), may hold values from -24 to 24
- queries: bfloat16 [49152, 4096], P(('rep', 'shard')), may hold values from -128 to 128
- keys: bfloat16 [49152, 512], P(('rep', 'shard')), may hold values from -5 to 5
- d_attn: bfloat16 [49152, 4096], P(('rep', 'shard')), may hold values from -6 to 6
- value_weight: bfloat16 [8192, 512], P('shard'), may hold values from -0.0625 to 0.0625
- pair_margin: float32 [256], P(('rep', 'shard')), may hold values from -30 to 30
- pair_chosen: int32 [256], P(('rep', 'shard')), may hold values from 0 to 1
Outputs:
- key_weight_grad: float32 [8192, 512], P('shard')
- value_weight_grad: float32 [8192, 512], P('shard')
The draws below stay inside these ranges and needn't reach their ends.
All inputs are finite; a program needn't handle non-finite values.
Results may differ from the reference program's by a relative error of at most 0.015.
Values may be sent and summed in bfloat16 or wider, within the bound.
A program may use at most 128 MiB of HBM per device.

```python
import math
import jax
import jax.numpy as jnp
from jax import lax

D = 8192
KVH = 4
GROUP = 8
HD = 128
LEN = 96
QH = 32
PAIRS = 256
TOKENS = 49152
N_REP = 32
N_SHARD = 8


def key_base(key):
    return jax.random.truncated_normal(jax.random.fold_in(key, 101), -4.0, 4.0, (TOKENS, KVH * HD), jnp.float32)


def draw_keys(key, part):
    base = key_base(key)
    return base.astype(jnp.bfloat16)


def draw_queries(key, part):
    key = jax.random.fold_in(key, 5)
    values = jax.random.truncated_normal(key, -4.0, 4.0, (TOKENS, KVH * GROUP * HD), jnp.float32)
    return values.astype(jnp.bfloat16)


def place_ends(array, key, low, high):
    longest = array.shape.index(max(array.shape))
    spots = []
    for shift in (0, 1):
        where = [jax.random.randint(jax.random.fold_in(key, axis), (), 0, length) for axis, length in enumerate(array.shape)]
        where[longest] = (where[longest] + shift) % array.shape[longest]
        spots.append(tuple(where))
    return array.at[spots[0]].set(low).at[spots[1]].set(high)


def spiked(array, own_key, source, target, parts, factor):
    owner, partner = [(jnp.arange(array.shape[dim]) // (array.shape[dim] // parts)).reshape([-1 if axis == dim else 1 for axis in range(array.ndim)]) for dim in (source, target)]
    chosen = jax.random.permutation(own_key, parts)[partner]
    strong = (owner == chosen) | (owner == (partner + parts // 2) % parts)
    return jnp.where(strong, factor * array, array)


def levels(stream_key, dims, pieces, least, top_value):
    loudness = 1.0
    for dim, shards_of in pieces:
        draws = jax.random.uniform(jax.random.fold_in(jax.random.fold_in(stream_key, 6), dim), (shards_of,), jnp.float32, least / len(pieces), top_value / len(pieces))
        loudness = loudness * jnp.repeat(jnp.exp(draws), dims[dim] // shards_of).reshape((-1,) + (1,) * (len(dims) - 1 - dim))
    return loudness


def scatter_about(key, dims, deviation, bound, split=(), kind=jnp.bfloat16):
    array = deviation * jax.random.normal(key, dims, jnp.float32)
    if split:
        array = array * levels(key, dims, split, -0.22, 0.18)
    return jnp.clip(array, -bound, bound).astype(kind)


def bell_draw_with(own_key, shape, spread, bound, shards, heavy, kind=jnp.bfloat16):
    values = spread * jax.random.normal(own_key, shape, jnp.float32)
    if shards:
        values = values * levels(own_key, shape, shards, -0.22, 0.18)
    return jnp.clip(spiked(values, jax.random.fold_in(own_key, 3), *heavy), -bound, bound).astype(kind)


def setup_inputs(seed: int = 0) -> dict:
    arg_keys = jax.random.split(jax.random.key(seed), 8)
    return {
        "hidden_in": bell_draw_with(arg_keys[0], (TOKENS, D), 1.0, 24.0, ((0, 256),), (0, 1, 256, 6.0)),
        "queries": draw_queries(jax.random.fold_in(arg_keys[7], 71), 0),
        "keys": draw_keys(jax.random.fold_in(arg_keys[7], 71), 0),
        "d_attn": scatter_about(arg_keys[3], (TOKENS, QH * HD), 1.0, 6.0, ((0, 256),)),
        "value_weight": scatter_about(arg_keys[4], (D, KVH * HD), D ** -0.5, 0.0625, ((0, 8),)),
        "pair_margin": jnp.clip(jax.random.uniform(arg_keys[5], (PAIRS,), jnp.float32, -30.0, 30.0) * levels(arg_keys[5], (PAIRS,), ((0, 256),), -0.4, 0.0), -30.0, 30.0),
        "pair_chosen": place_ends(jax.random.randint(arg_keys[6], (PAIRS,), 0, 2), jax.random.fold_in(arg_keys[6], 1), 0, 1).astype(jnp.int32),
    }


BETA_SPIN = 0.1
ROPE_BASE = 500000.0

def rotate_back(grad, positions):
    half = grad.shape[-1] // 2
    freqs = ROPE_BASE ** (-2.0 * jnp.arange(half, dtype=jnp.float32) / grad.shape[-1])
    angles = positions.astype(jnp.float32)[:, None] * freqs[None, :]
    cosine = jnp.cos(angles)[:, None, :]
    sine = jnp.sin(angles)[:, None, :]
    first = grad[..., :half]
    second = grad[..., half:]
    return jnp.concatenate([first * cosine + second * sine, second * cosine - first * sine], axis=-1)

def token_weights(pair_margin, pair_chosen):
    strength = BETA_SPIN * jax.nn.sigmoid(-BETA_SPIN * pair_margin)
    first = strength * (2 * pair_chosen - 1).astype(jnp.float32)
    both = jnp.stack([first, -first], axis=1)
    return jnp.broadcast_to(both[:, :, None], (both.shape[0], 2, LEN)).reshape(-1)

def device_grads(xrows, queries, keys, d_attn, seq_weight, value_weight):
    tok = xrows.shape[0]
    score_scale = 1.0 / math.sqrt(HD)
    position = jnp.arange(tok, dtype=jnp.int32)
    local_pos = position % LEN
    same = position[:, None] // LEN == position[None, :] // LEN
    allowed = same & (local_pos[None, :] <= local_pos[:, None])
    values = jnp.dot(xrows, value_weight, preferred_element_type=jnp.float32).astype(jnp.bfloat16)
    query_head_rows = queries.astype(jnp.float32).reshape(tok, KVH, GROUP, HD)
    key_head_rows = keys.astype(jnp.float32).reshape(tok, KVH, HD)
    attention_scores = jnp.einsum('zvkj,ovj->vkzo', query_head_rows, key_head_rows) * score_scale
    attention_scores = jnp.where(allowed, attention_scores, -jnp.inf)
    top = lax.optimization_barrier(jnp.max(attention_scores, axis=-1, keepdims=True))
    expo = jnp.exp(attention_scores - top)
    probs = expo / lax.optimization_barrier(jnp.sum(expo, axis=-1, keepdims=True))
    probability_narrow = probs.astype(jnp.bfloat16)
    scaled = (d_attn.astype(jnp.float32) * seq_weight[:, None]).astype(jnp.bfloat16)
    scaled_query_heads = scaled.astype(jnp.float32).reshape(tok, KVH, GROUP, HD)
    values_gradient = jnp.einsum('fceq,efcb->qfb', probability_narrow.astype(jnp.float32), scaled_query_heads)
    values_gradient = values_gradient.reshape(tok, KVH * HD).astype(jnp.bfloat16)
    value_head_rows = values.astype(jnp.float32).reshape(tok, KVH, HD)
    probability_gradient = jnp.einsum('zvkj,ovj->vkzo', scaled_query_heads, value_head_rows)
    inner = lax.optimization_barrier(jnp.sum(probs * probability_gradient, axis=-1, keepdims=True))
    score_gradient = (probs * (probability_gradient - inner) * score_scale).astype(jnp.bfloat16)
    rotated_gradient = jnp.einsum('fceq,efcb->qfb', score_gradient.astype(jnp.float32), query_head_rows)
    d_keys = rotate_back(rotated_gradient, local_pos).reshape(tok, KVH * HD).astype(jnp.bfloat16)
    part_key = jnp.dot(xrows.T, d_keys, preferred_element_type=jnp.float32).astype(jnp.bfloat16)
    part_value = jnp.dot(xrows.T, values_gradient, preferred_element_type=jnp.float32).astype(jnp.bfloat16)
    part_key = lax.optimization_barrier(part_key)
    part_value = lax.optimization_barrier(part_value)
    return (part_key.astype(jnp.float32), part_value.astype(jnp.float32))

def reference(hidden_in, queries, keys, d_attn, value_weight, pair_margin, pair_chosen):
    count = N_REP * N_SHARD
    tok = 2 * LEN
    seq_weight = token_weights(pair_margin, pair_chosen)
    inputs = (hidden_in.reshape(count, tok, D), queries.reshape(count, tok, QH * HD), keys.reshape(count, tok, KVH * HD), d_attn.reshape(count, tok, QH * HD), seq_weight.reshape(count, tok))

    def step(carry, item):
        part_key, part_value = device_grads(item[0], item[1], item[2], item[3], item[4], value_weight)
        return ((carry[0] + part_key, carry[1] + part_value), None)
    start = (jnp.zeros((D, KVH * HD), jnp.float32), jnp.zeros((D, KVH * HD), jnp.float32))
    totals, unused = lax.scan(step, start, inputs)
    return (totals[0], totals[1])
```

```python
import functools
import math

import jax
import jax.numpy as jnp
import numpy as np
from jax import lax
from jax.experimental import pallas as pl
from jax.experimental.pallas import tpu as pltpu
from jax.sharding import PartitionSpec as P

HD = 128
LEN = 96
TOK = 192
HEADS = 4
GROUP = 8
COLS = GROUP * LEN
BETA_SPIN = 0.1
ROPE_BASE = 500000.0
SCALE = 1.0 / math.sqrt(HD)
MESH = pl.DeviceIdType.MESH
BF = jnp.bfloat16
F32 = jnp.float32


class Links:
    def __init__(self, send, recv):
        self.send, self.recv, self.count, self.all = send, recv, 0, []

    def start(self, src, dst, device):
        copy = pltpu.make_async_remote_copy(
            src_ref=src,
            dst_ref=dst,
            send_sem=self.send.at[self.count],
            recv_sem=self.recv.at[self.count],
            device_id=device,
            device_id_type=MESH,
        )
        copy.start()
        self.count += 1
        self.all.append(copy)
        return copy


def kernel(
    margin, chosen, cosine, sine, q, k, da, x_hbm, wv_hbm,
    out_k, out_v,
    xc, wc, probs, sc, qc, acc, vr, vals, dvb, dkb,
    pv, rz0, rz, rvx, vx, rvy,
    pa, ra1, ra2, qa, ra3, ra4,
    pb, rb1, rb2, qb, rb3, rb4,
    kz, rkz, send, recv, local,
):
    rep, shard = lax.axis_index("rep"), lax.axis_index("shard")
    z, l, c = rep // 4, (rep // 2) % 2, rep % 2
    h, y = shard // 4, shard % 4
    x = 2 * h + l

    def dev(xx, yy, zz, cc):
        return (zz * 4 + (xx % 2) * 2 + cc, (xx // 2) * 4 + yy)

    def at_x(d):
        return dev((x + d) % 4, y, z, c)

    def at_y(d):
        return dev(x, (y + d) % 4, z, c)

    def at_z(d):
        return dev(x, y, (z + d) % 8, c)

    sib = dev(x, y, z, 1 - c)
    outer = dev(3 - x, y, z, c)
    inner = dev(2 * h + 1 - l, y, z, c)

    peers = [sib] + [at_x(d) for d in (1, 2, 3)] + [at_y(d) for d in (1, 2, 3)] + [at_z(d) for d in range(1, 8)]
    barrier = pltpu.get_barrier_semaphore()
    for peer in peers:
        pl.semaphore_signal(barrier, inc=1, device_id=peer, device_id_type=MESH)
    pl.semaphore_wait(barrier, len(peers))

    links = Links(send, recv)

    def rows_of(quarter):
        return pl.ds(pl.multiple_of(quarter * 512 + c * 256, 256), 256)

    own_copies = []

    def keep(src, dst):
        copy = pltpu.make_async_copy(src, dst, local.at[len(own_copies)])
        copy.start()
        own_copies.append(copy)

    first = 1 - l
    w_outer = {0: links.start(wv_hbm.at[rows_of(first)], wc.at[(2 * h + first) * 4 + y], outer)}
    w_y = {}
    for quarter in (first, l):
        for d in (1, 3, 2):
            w_y[d, quarter is first] = links.start(
                wv_hbm.at[rows_of(quarter)], wc.at[(2 * h + quarter) * 4 + y], at_y(d)
            )
    xs = []
    for xx in range(4):
        for yy in range(4):
            base = (xx // 2) * 4096 + yy * 1024 + (xx % 2) * 512
            theirs = pl.ds(pl.multiple_of(base + (1 - c) * 256, 256), 256)
            mine = pl.ds(pl.multiple_of(base + c * 256, 256), 256)
            xs.append(links.start(x_hbm.at[:, theirs], xc.at[xx * 4 + yy, c], sib))
            keep(x_hbm.at[:, mine], xc.at[xx * 4 + yy, c])
    for quarter in range(2):
        keep(wv_hbm.at[rows_of(quarter)], wc.at[(2 * h + quarter) * 4 + y])

    strength = BETA_SPIN / (1.0 + jnp.exp(BETA_SPIN * margin[...]))
    weight = strength * (2 * chosen[...] - 1).astype(F32)
    s_pos = lax.broadcasted_iota(jnp.int32, (LEN, COLS), 0)
    t_pos = lax.broadcasted_iota(jnp.int32, (LEN, COLS), 1) % LEN
    allowed = s_pos <= t_pos

    def forward(g, carry):
        for seq in range(2):
            unit = 2 * g + seq
            rows = pl.ds(seq * LEN, LEN)
            w = weight if seq == 0 else -weight
            for head in range(GROUP):
                cols = pl.ds(pl.multiple_of(g * GROUP * HD + head * HD, HD), HD)
                span = pl.ds(head * LEN, LEN)
                qc[unit, span, :] = q[rows, cols]
                sc[unit, span, :] = (da[rows, cols].astype(F32) * w).astype(BF)
            kcols = pl.ds(pl.multiple_of(g * HD, HD), HD)
            scores = lax.dot_general(
                k[rows, kcols], qc[unit], (((1,), (1,)), ((), ())), preferred_element_type=F32
            ) * SCALE
            scores = jnp.where(allowed, scores, -jnp.inf)
            top = jnp.max(scores, axis=0, keepdims=True)
            expo = jnp.exp(scores - top)
            p = expo / jnp.sum(expo, axis=0, keepdims=True)
            probs[unit] = p
            dv = jnp.dot(p.astype(BF), sc[unit], preferred_element_type=F32)
            dvb[c, rows, kcols] = dv.astype(BF)
        return carry

    lax.fori_loop(0, HEADS, forward, 0)
    dv_copy = links.start(dvb.at[c], dvb.at[c], sib)
    for copy in own_copies:
        copy.wait()
    for copy in xs:
        copy.wait_recv()
    dv_copy.wait_recv()

    def partial_grad(d, store):
        dt = jnp.transpose(d[...].reshape(2 * TOK, 512).astype(F32)).astype(BF)

        def body(i, carry):
            out = jnp.dot(dt, xc[i].reshape(2 * TOK, 256), preferred_element_type=F32).astype(BF)
            for zz in range(8):
                cb, rh = zz // 2, zz % 2
                store(i, zz, out[cb * 128 : (cb + 1) * 128, rh * 128 : (rh + 1) * 128])
            return carry

        lax.fori_loop(0, 16, body, 0)

    def store_v(i, zz, block):
        pv[zz, i] = block

    partial_grad(dvb, store_v)

    half_a, half_b = pl.ds(0, 8), pl.ds(8, 8)

    def add(dst, src, start, count):
        def body(i, carry):
            dst[start + i] = (dst[start + i].astype(F32) + src[i].astype(F32)).astype(BF)
            return carry

        lax.fori_loop(0, count, body, 0)

    def z_at(d):
        return pv.at[(z + d) % 8]

    z_copies = {}

    def z_step(step):
        for di, sign in ((0, 1), (1, -1)):
            lead, other = (half_a, half_b) if sign == 1 else (half_b, half_a)
            lead0, other0 = (0, 8) if sign == 1 else (8, 0)
            far = z_at(sign * (4 - step) + 8)
            near = z_at(sign * (3 - step) + 8)
            if step > 0:
                z_copies[di, step - 1, 0].wait_recv()
                add(far, rz.at[di, step - 1, half_a], lead0, 8)
            z_copies[di, step, 0] = links.start(far.at[lead], rz.at[di, step, half_a], at_z(sign + 8))
            if step < 3:
                if step > 0:
                    z_copies[di, step - 1, 1].wait_recv()
                    add(near, rz.at[di, step - 1, half_b], other0, 8)
                z_copies[di, step, 1] = links.start(near.at[other], rz.at[di, step, half_b], at_z(sign + 8))

    z_step(0)

    def values_add(count, place, init=False):
        def body(i, carry):
            j = place(i)
            part = jnp.dot(
                xc[j].reshape(2 * TOK, 256), wc[j], preferred_element_type=F32
            ).reshape(2, TOK, 512)
            acc[...] += part
            return carry

        lax.fori_loop(0, count, body, 0)

    def pass_outer(d):
        w_y[d, True].wait_recv()
        block = wc.at[(2 * h + first) * 4 + (y + 4 - d) % 4]
        w_outer[d] = links.start(block, block, outer)

    w_inner = {}

    def pass_inner(d):
        w_outer[d].wait_recv()
        block = wc.at[(2 * (1 - h) + l) * 4 + (y + 4 - d) % 4]
        w_inner[d] = links.start(block, block, inner)

    acc[...] = jnp.zeros_like(acc)
    pass_inner(0)
    pass_outer(1)
    pass_outer(3)
    pass_outer(2)
    values_add(2, lambda i: (2 * h + i) * 4 + y)
    pass_inner(1)
    z_step(1)
    pass_inner(3)
    for d in (1, 3, 2):
        w_y[d, False].wait_recv()
    values_add(6, lambda i: (2 * h + i % 2) * 4 + (y + 1 + i // 2) % 4)
    pass_inner(2)
    values_add(4, lambda i: (2 * (1 - h) + l) * 4 + i)
    for d in (0, 1, 3, 2):
        w_inner[d].wait_recv()
    values_add(4, lambda i: (2 * (1 - h) + 1 - l) * 4 + i)
    value_copy = links.start(acc.at[1 - c], vr, sib)
    z_step(2)
    value_copy.wait_recv()
    vals[...] = (acc[c] + vr[...]).astype(BF)

    def backward(g, carry):
        for seq in range(2):
            unit = 2 * g + seq
            rows = pl.ds(seq * LEN, LEN)
            kcols = pl.ds(pl.multiple_of(g * HD, HD), HD)
            dp = lax.dot_general(
                vals[rows, kcols], sc[unit], (((1,), (1,)), ((), ())), preferred_element_type=F32
            )
            p = probs[unit]
            mean = jnp.sum(p * dp, axis=0, keepdims=True)
            ds = (p * (dp - mean) * SCALE).astype(BF)
            rot = jnp.dot(ds, qc[unit], preferred_element_type=F32)
            swapped = jnp.concatenate([rot[:, HD // 2 :], rot[:, : HD // 2]], axis=1)
            dkb[c, rows, kcols] = (rot * cosine[...] + swapped * sine[...]).astype(BF)
        return carry

    lax.fori_loop(0, HEADS, backward, 0)
    dk_copy = links.start(dkb.at[c], dkb.at[c], sib)
    dk_copy.wait_recv()

    def store_k(i, zz, block):
        pa[i // 4, i % 4, zz] = block[:64]
        pb[i % 4, i // 4, zz] = block[64:]

    partial_grad(dkb, store_k)

    def ring_start(at, me, p, r1, r2, n):
        lo, hi = pl.ds(0, n // 2), pl.ds(n // 2, n // 2)
        far, up, down = p.at[(me + 2) % 4], p.at[(me + 1) % 4], p.at[(me + 3) % 4]
        return {
            "up1": links.start(far.at[lo], r1.at[0], at(1)),
            "down1": links.start(far.at[hi], r1.at[1], at(3)),
            "up2": links.start(up.at[hi], r2.at[0, hi], at(1)),
            "down2": links.start(down.at[lo], r2.at[1, lo], at(3)),
        }

    def add2(dst, src, start, count):
        def body(i, carry):
            dst[start + i] = (dst[start + i].astype(F32) + src[i].astype(F32)).astype(BF)
            return carry

        lax.fori_loop(0, count, body, 0)

    def ring_pass(copies, at, me, p, r1, r2, n):
        lo, hi = pl.ds(0, n // 2), pl.ds(n // 2, n // 2)
        up, down = p.at[(me + 1) % 4], p.at[(me + 3) % 4]
        copies["up1"].wait_recv()
        add2(up, r1.at[0], 0, n // 2)
        copies["up3"] = links.start(up.at[lo], r2.at[0, lo], at(1))
        copies["down1"].wait_recv()
        add2(down, r1.at[1], n // 2, n // 2)
        copies["down3"] = links.start(down.at[hi], r2.at[1, hi], at(3))

    def ring_end(copies, me, p, r2, n, store):
        for name in ("up2", "down2", "up3", "down3"):
            copies[name].wait_recv()

        def body(i, carry):
            store(i, p[me, i].astype(F32) + r2[0, i].astype(F32) + r2[1, i].astype(F32))
            return carry

        lax.fori_loop(0, n, body, 0)

    a1 = ring_start(at_x, x, pa, ra1, ra2, 4)
    b1 = ring_start(at_y, y, pb, rb1, rb2, 4)
    z_step(3)
    ring_pass(a1, at_x, x, pa, ra1, ra2, 4)
    ring_pass(b1, at_y, y, pb, rb1, rb2, 4)

    z_copies[0, 2, 1].wait_recv()
    z_copies[1, 2, 1].wait_recv()
    z_copies[0, 3, 0].wait_recv()
    z_copies[1, 3, 0].wait_recv()
    mine = z_at(0)

    def v_sum(i, carry):
        lead_up, other_up = rz[0, 3, i % 8], rz[0, 2, 8 + i % 8]
        lead_down, other_down = rz[1, 3, i % 8], rz[1, 2, 8 + i % 8]
        in_a = i < 8
        up = jnp.where(in_a, lead_up.astype(F32), other_up.astype(F32))
        down = jnp.where(in_a, other_down.astype(F32), lead_down.astype(F32))
        mine[i] = (mine[i].astype(F32) + up + down).astype(BF)
        return carry

    lax.fori_loop(0, 16, v_sum, 0)
    vx_copies = [
        links.start(mine.at[pl.ds(((x + d) % 4) * 4, 4)], rvx.at[d - 1], at_x(d)) for d in (1, 2, 3)
    ]

    def store_qa(i, total):
        qa[i] = total.astype(BF)

    def store_qb(i, total):
        qb[i] = total.astype(BF)

    ring_end(a1, x, pa, ra2, 4, store_qa)
    a2 = ring_start(at_y, y, qa, ra3, ra4, 8)
    ring_end(b1, y, pb, rb2, 4, store_qb)
    b2 = ring_start(at_x, x, qb, rb3, rb4, 8)

    for copy in vx_copies:
        copy.wait_recv()

    def vx_sum(i, carry):
        total = mine[x * 4 + i].astype(F32)
        for d in range(3):
            total += rvx[d, i].astype(F32)
        vx[i] = total.astype(BF)
        return carry

    lax.fori_loop(0, 4, vx_sum, 0)
    vy_copies = [links.start(vx.at[(y + d) % 4], rvy.at[d - 1], at_y(d)) for d in (1, 2, 3)]

    ring_pass(a2, at_y, y, qa, ra3, ra4, 8)
    ring_pass(b2, at_x, x, qb, rb3, rb4, 8)

    def spot(ref, zz, ll, cc):
        row = ll * 512 + cc * 256 + (zz % 2) * 128
        return ref.at[
            pl.ds(pl.multiple_of(row, 128), 128), pl.ds(pl.multiple_of((zz // 2) * 128, 128), 128)
        ]

    def gather_start(ref, total):
        place = spot(ref, z, l, c)
        place[...] = jnp.transpose(total).astype(BF)
        state = {"z": {}, "in": {}, "sib": {}}
        for d in (4, 3, 5, 2, 6, 1, 7):
            state["z"][d] = links.start(place, place, at_z(d))
        state["in"][0] = links.start(place, place, inner)
        state["sib"][0, 0] = links.start(place, place, sib)
        return state

    def gather_mid(ref, state):
        for d in (1, 7, 2, 6, 3, 5, 4):
            state["z"][d].wait_recv()
            place = spot(ref, (z + 8 - d) % 8, l, c)
            state["in"][d] = links.start(place, place, inner)
            state["sib"][d, 0] = links.start(place, place, sib)

    def gather_end(ref, state):
        for d in (0, 1, 7, 2, 6, 3, 5, 4):
            state["in"][d].wait_recv()
            place = spot(ref, (z + 8 - d) % 8, 1 - l, c)
            state["sib"][d, 1] = links.start(place, place, sib)

    for copy in vy_copies:
        copy.wait_recv()
    total_v = vx[y].astype(F32)
    for d in range(3):
        total_v += rvy[d].astype(F32)
    gv = gather_start(out_v, total_v)

    def store_za(i, total):
        kz[i, pl.ds(0, 64), :] = total.astype(BF)

    def store_zb(i, total):
        kz[i, pl.ds(64, 64), :] = total.astype(BF)

    ring_end(a2, y, qa, ra4, 8, store_za)
    ring_end(b2, x, qb, rb4, 8, store_zb)
    kz_copies = [links.start(kz.at[(z + d) % 8], rkz.at[d - 1], at_z(d)) for d in range(1, 8)]
    gather_mid(out_v, gv)
    total_k = kz[z].astype(F32)
    for d in range(7):
        kz_copies[d].wait_recv()
        total_k += rkz[d].astype(F32)
    gk = gather_start(out_k, total_k)
    gather_end(out_v, gv)
    gather_mid(out_k, gk)
    gather_end(out_k, gk)
    for state in (gv, gk):
        for copy in state["sib"].values():
            copy.wait_recv()
    for copy in links.all:
        copy.wait_send()


def rotary_tables():
    half = HD // 2
    freqs = np.float32(ROPE_BASE) ** (-2.0 * np.arange(half, dtype=np.float32) / HD)
    angles = np.arange(LEN, dtype=np.float32)[:, None] * freqs.astype(np.float32)[None, :]
    cosine, sine = np.cos(angles), np.sin(angles)
    return (
        np.concatenate([cosine, cosine], axis=1).astype(np.float32),
        np.concatenate([sine, -sine], axis=1).astype(np.float32),
    )


def shards(hidden_in, queries, keys, d_attn, value_weight, pair_margin, pair_chosen):
    cosine, sine = rotary_tables()
    vmem = pl.BlockSpec(memory_space=pltpu.VMEM)
    anywhere = pl.BlockSpec(memory_space=pl.ANY)
    block = (128, 128)
    key_grad, value_grad = pl.pallas_call(
        kernel,
        name="projection_grads",
        out_shape=[jax.ShapeDtypeStruct((1024, 512), BF)] * 2,
        in_specs=[vmem] * 7 + [anywhere] * 2,
        out_specs=[vmem] * 2,
        scratch_shapes=[
            pltpu.VMEM((16, 2, TOK, 256), BF),
            pltpu.VMEM((16, 256, 512), BF),
            pltpu.VMEM((8, LEN, COLS), F32),
            pltpu.VMEM((8, COLS, HD), BF),
            pltpu.VMEM((8, COLS, HD), BF),
            pltpu.VMEM((2, TOK, 512), F32),
            pltpu.VMEM((TOK, 512), F32),
            pltpu.VMEM((TOK, 512), BF),
            pltpu.VMEM((2, TOK, 512), BF),
            pltpu.VMEM((2, TOK, 512), BF),
            pltpu.VMEM((8, 16) + block, BF),
            pltpu.VMEM((1, 128), BF),
            pltpu.VMEM((2, 4, 16) + block, BF),
            pltpu.VMEM((3, 4) + block, BF),
            pltpu.VMEM((4,) + block, BF),
            pltpu.VMEM((3,) + block, BF),
        ]
        + [
            pltpu.VMEM((4, 4, 8, 64, 128), BF),
            pltpu.VMEM((2, 2, 8, 64, 128), BF),
            pltpu.VMEM((2, 4, 8, 64, 128), BF),
            pltpu.VMEM((4, 8, 64, 128), BF),
            pltpu.VMEM((2, 4, 64, 128), BF),
            pltpu.VMEM((2, 8, 64, 128), BF),
        ]
        * 2
        + [
            pltpu.VMEM((8,) + block, BF),
            pltpu.VMEM((7,) + block, BF),
            pltpu.SemaphoreType.DMA((160,)),
            pltpu.SemaphoreType.DMA((160,)),
            pltpu.SemaphoreType.DMA((18,)),
        ],
        compiler_params=pltpu.CompilerParams(
            collective_id=0, has_side_effects=True, vmem_limit_bytes=58 * 2**20
        ),
    )(
        pair_margin.reshape(1, 1),
        pair_chosen.reshape(1, 1),
        jnp.asarray(cosine),
        jnp.asarray(sine),
        queries,
        keys,
        d_attn,
        hidden_in,
        value_weight,
    )
    return key_grad.astype(F32), value_grad.astype(F32)


def solution(mesh):
    placed = (
        P(("rep", "shard"), None),
        P(("rep", "shard"), None),
        P(("rep", "shard"), None),
        P(("rep", "shard"), None),
        P("shard", None),
        P(("rep", "shard")),
        P(("rep", "shard")),
    )
    return jax.shard_map(
        shards,
        mesh=mesh,
        in_specs=placed,
        out_specs=(P("shard", None), P("shard", None)),
        check_vma=False,
    )
```

```python
import functools
import math

import jax
import jax.numpy as jnp
import numpy as np
from jax import lax
from jax.experimental import pallas as pl
from jax.experimental.pallas import tpu as pltpu
from jax.sharding import PartitionSpec as P

HD = 128
LEN = 96
TOK = 192
HEADS = 4
GROUP = 8
COLS = GROUP * LEN
BETA_SPIN = 0.1
ROPE_BASE = 500000.0
SCALE = 1.0 / math.sqrt(HD)
MESH = pl.DeviceIdType.MESH
BF = jnp.bfloat16
F32 = jnp.float32


class Links:
    def __init__(self, send, recv):
        self.send, self.recv, self.count, self.all = send, recv, 0, []

    def start(self, src, dst, device):
        copy = pltpu.make_async_remote_copy(
            src_ref=src,
            dst_ref=dst,
            send_sem=self.send.at[self.count],
            recv_sem=self.recv.at[self.count],
            device_id=device,
            device_id_type=MESH,
        )
        copy.start()
        self.count += 1
        self.all.append(copy)
        return copy


def add_blocks(dst, src, count):
    for i in range(count):
        dst[i] = (dst[i].astype(F32) + src[i].astype(F32)).astype(BF)


def kernel(
    margin, chosen, cos_hbm, sin_hbm, q_hbm, k_hbm, da_hbm, x_hbm, wv_hbm,
    out_k, out_v,
    cosine, sine, q, k, da,
    xc, wc, probs, sc, qc, acc, vr, vals, dvb, dkb,
    pv, rz, va1, va2, va3, vb1, vb2, vb3,
    pa, ra1, ra2, qa, ra3,
    pb, rb1, rb2, qb, rb3,
    kz, rkz, send, recv, local, kz_send, kz_recv,
):
    rep, shard = lax.axis_index("rep"), lax.axis_index("shard")
    z, l, c = rep // 4, (rep // 2) % 2, rep % 2
    h, y = shard // 4, shard % 4
    x = 2 * h + l

    def dev(xx, yy, zz, cc):
        return (zz * 4 + (xx % 2) * 2 + cc, (xx // 2) * 4 + yy)

    def at_x(d):
        return dev((x + d) % 4, y, z, c)

    def at_y(d):
        return dev(x, (y + d) % 4, z, c)

    def at_z(d):
        return dev(x, y, (z + d) % 8, c)

    sib = dev(x, y, z, 1 - c)
    outer = dev(3 - x, y, z, c)
    inner = dev(2 * h + 1 - l, y, z, c)

    peers = [sib] + [at_x(d) for d in (1, 2, 3)] + [at_y(d) for d in (1, 2, 3)] + [at_z(d) for d in range(1, 8)]
    barrier = pltpu.get_barrier_semaphore()
    for peer in peers:
        pl.semaphore_signal(barrier, inc=1, device_id=peer, device_id_type=MESH)

    kept = []

    def keep(src, dst):
        copy = pltpu.make_async_copy(src, dst, local.at[len(kept)])
        copy.start()
        kept.append(copy)

    def rows_of(quarter):
        return pl.ds(pl.multiple_of(quarter * 512 + c * 256, 256), 256)

    def columns_of(xx, yy, core):
        return pl.ds(pl.multiple_of((xx // 2) * 4096 + yy * 1024 + (xx % 2) * 512 + core * 256, 256), 256)

    for src, dst in ((q_hbm, q), (k_hbm, k), (da_hbm, da), (cos_hbm, cosine), (sin_hbm, sine)):
        keep(src, dst)
    for xx in range(4):
        for yy in range(4):
            keep(x_hbm.at[:, columns_of(xx, yy, c)], xc.at[xx * 4 + yy, c])
    for quarter in range(2):
        keep(wv_hbm.at[rows_of(quarter)], wc.at[(2 * h + quarter) * 4 + y])

    pl.semaphore_wait(barrier, len(peers))

    links = Links(send, recv)
    first = 1 - l
    w_outer = {0: links.start(wv_hbm.at[rows_of(first)], wc.at[(2 * h + first) * 4 + y], outer)}
    w_y = {}
    for quarter in (first, l):
        for d in (1, 3, 2):
            w_y[d, quarter is first] = links.start(
                wv_hbm.at[rows_of(quarter)], wc.at[(2 * h + quarter) * 4 + y], at_y(d)
            )
    xs = []
    for xx in range(4):
        for yy in range(4):
            xs.append(links.start(x_hbm.at[:, columns_of(xx, yy, 1 - c)], xc.at[xx * 4 + yy, c], sib))

    strength = BETA_SPIN / (1.0 + jnp.exp(BETA_SPIN * margin[...]))
    weight = strength * (2 * chosen[...] - 1).astype(F32)
    s_pos = lax.broadcasted_iota(jnp.int32, (LEN, COLS), 0)
    t_pos = lax.broadcasted_iota(jnp.int32, (LEN, COLS), 1) % LEN
    allowed = s_pos <= t_pos
    for copy in kept[:5]:
        copy.wait()

    def forward(g):
        for seq in range(2):
            unit = 2 * g + seq
            rows = pl.ds(seq * LEN, LEN)
            w = weight if seq == 0 else -weight
            for head in range(GROUP):
                cols = pl.ds((g * GROUP + head) * HD, HD)
                span = pl.ds(head * LEN, LEN)
                qc[unit, span, :] = q[rows, cols]
                sc[unit, span, :] = (da[rows, cols].astype(F32) * w).astype(BF)
            kcols = pl.ds(g * HD, HD)
            scores = lax.dot_general(
                k[rows, kcols], qc[unit], (((1,), (1,)), ((), ())), preferred_element_type=F32
            ) * SCALE
            scores = jnp.where(allowed, scores, -jnp.inf)
            top = jnp.max(scores, axis=0, keepdims=True)
            expo = jnp.exp(scores - top)
            p = expo / jnp.sum(expo, axis=0, keepdims=True)
            probs[unit] = p
            dv = jnp.dot(p.astype(BF), sc[unit], preferred_element_type=F32)
            dvb[c, rows, kcols] = dv.astype(BF)

    for g in range(HEADS):
        forward(g)
    dv_copy = links.start(dvb.at[c], dvb.at[c], sib)
    for copy in kept[5:]:
        copy.wait()
    for copy in xs:
        copy.wait_recv()
    dv_copy.wait_recv()

    dt = jnp.transpose(dvb[...].reshape(2 * TOK, 512).astype(F32)).astype(BF)

    def grad_v(xx, carry):
        for yy in range(4):
            out = jnp.dot(dt, xc[xx * 4 + yy].reshape(2 * TOK, 256), preferred_element_type=F32).astype(BF)
            for zz in range(8):
                cb, rh = zz // 2, zz % 2
                pv[zz, xx, yy] = out[cb * 128 : (cb + 1) * 128, rh * 128 : (rh + 1) * 128]
        return carry

    lax.fori_loop(0, 4, grad_v, 0)

    half_a, half_b = pl.ds(0, 2), pl.ds(2, 2)

    def z_at(d):
        return pv.at[(z + d + 8) % 8]

    z_copies = {}

    def z_add(dst, src):
        for i in range(2):
            add_blocks(dst.at[i], src.at[i], 4)

    def z_step(step):
        for di, sign in ((0, 1), (1, -1)):
            lead, other = (half_a, half_b) if sign == 1 else (half_b, half_a)
            far = z_at(sign * (4 - step)).at[lead]
            near = z_at(sign * (3 - step)).at[other]
            if step > 0:
                z_copies[di, step - 1, 0].wait_recv()
                z_add(far, rz.at[di, step - 1, half_a])
            z_copies[di, step, 0] = links.start(far, rz.at[di, step, half_a], at_z(sign + 8))
            if step < 3:
                if step > 0:
                    z_copies[di, step - 1, 1].wait_recv()
                    z_add(near, rz.at[di, step - 1, half_b])
                z_copies[di, step, 1] = links.start(near, rz.at[di, step, half_b], at_z(sign + 8))

    z_step(0)

    def product(tokens, indices):
        total = None
        for j in indices:
            left = xc[j].reshape(2 * TOK, 256) if tokens is None else xc[j, tokens]
            part = jnp.dot(left, wc[j], preferred_element_type=F32)
            total = part if total is None else total + part
        return total

    def pass_outer(d):
        w_y[d, True].wait_recv()
        block = wc.at[(2 * h + first) * 4 + (y + 4 - d) % 4]
        w_outer[d] = []
        parts = 4 if d == 2 else 2
        for part in range(parts):
            piece = block.at[pl.ds(part * (256 // parts), 256 // parts)]
            w_outer[d].append(links.start(piece, piece, outer))

    w_inner = []

    def pass_inner(d):
        block = wc.at[(2 * (1 - h) + l) * 4 + (y + 4 - d) % 4]
        copies = w_outer[d] if d else [w_outer[0]]
        for part, copy in enumerate(copies):
            copy.wait_recv()
            size = 256 // len(copies)
            piece = block.at[pl.ds(part * size, size)]
            w_inner.append(links.start(piece, piece, inner))

    pass_outer(1)
    pass_outer(3)
    pass_inner(0)
    acc[...] = product(None, [(2 * h + i) * 4 + y for i in range(2)]).reshape(2, TOK, 512)
    pass_outer(2)
    pass_inner(1)
    z_step(1)
    pass_inner(3)
    for d in (1, 3, 2):
        w_y[d, False].wait_recv()
    acc[...] += product(
        None, [(2 * h + i % 2) * 4 + (y + 1 + i // 2) % 4 for i in range(6)]
    ).reshape(2, TOK, 512)
    pass_inner(2)
    acc[...] += product(None, [(2 * (1 - h) + l) * 4 + i for i in range(4)]).reshape(2, TOK, 512)
    for copy in w_inner:
        copy.wait_recv()
    last = [(2 * (1 - h) + 1 - l) * 4 + i for i in range(4)]
    acc[1 - c] += product(1 - c, last)
    value_copy = links.start(acc.at[1 - c], vr, sib)
    acc[c] += product(c, last)
    z_step(2)
    value_copy.wait_recv()
    vals[...] = (acc[c] + vr[...]).astype(BF)

    dk_copies = {}

    def backward(g):
        kcols = pl.ds(g * HD, HD)
        for seq in range(2):
            unit = 2 * g + seq
            rows = pl.ds(seq * LEN, LEN)
            dp = lax.dot_general(
                vals[rows, kcols], sc[unit], (((1,), (1,)), ((), ())), preferred_element_type=F32
            )
            p = probs[unit]
            mean = jnp.sum(p * dp, axis=0, keepdims=True)
            ds = (p * (dp - mean) * SCALE).astype(BF)
            rot = jnp.dot(ds, qc[unit], preferred_element_type=F32)
            swapped = jnp.concatenate([rot[:, HD // 2 :], rot[:, : HD // 2]], axis=1)
            dkb[g, c, rows, :] = (rot * cosine[...] + swapped * sine[...]).astype(BF)
        dk_copies[g] = links.start(dkb.at[g, c], dkb.at[g, c], sib)

    def grad_k(g):
        dk_copies[g].wait_recv()
        dt = jnp.transpose(dkb[g].reshape(2 * TOK, HD).astype(F32)).astype(BF)
        for i in range(16):
            out = jnp.dot(dt, xc[i].reshape(2 * TOK, 256), preferred_element_type=F32).astype(BF)
            for rh in range(2):
                pa[g, i // 4, i % 4, rh] = out[:64, rh * 128 : (rh + 1) * 128]
                pb[g, i % 4, i // 4, rh] = out[64:, rh * 128 : (rh + 1) * 128]

    stream_a = (at_x, x, pa, ra1, ra2, qa, at_y, y, ra3)
    stream_b = (at_y, y, pb, rb1, rb2, qb, at_x, x, rb3)
    lo, hi = pl.ds(0, 2), pl.ds(2, 2)
    ring = {}

    def ring_start(g):
        for name, (at, me, p, r1, r2, _, _, _, _) in (("a", stream_a), ("b", stream_b)):
            far = p.at[g, (me + 2) % 4]
            ring[g, name, "up1"] = links.start(far.at[lo], r1.at[g, 0], at(1))
            ring[g, name, "down1"] = links.start(far.at[hi], r1.at[g, 1], at(3))
        for name, (at, me, p, r1, r2, _, _, _, _) in (("a", stream_a), ("b", stream_b)):
            up, down = p.at[g, (me + 1) % 4], p.at[g, (me + 3) % 4]
            ring[g, name, "up2"] = links.start(up.at[hi], r2.at[g, 0, hi], at(1))
            ring[g, name, "down2"] = links.start(down.at[lo], r2.at[g, 1, lo], at(3))

    def ring_pass(g):
        for name, (at, me, p, r1, r2, _, _, _, _) in (("a", stream_a), ("b", stream_b)):
            up, down = p.at[g, (me + 1) % 4].at[lo], p.at[g, (me + 3) % 4].at[hi]
            ring[g, name, "up1"].wait_recv()
            for i in range(2):
                add_blocks(up.at[i], r1.at[g, 0, i], 2)
            ring[g, name, "up3"] = links.start(up, r2.at[g, 0, lo], at(1))
            ring[g, name, "down1"].wait_recv()
            for i in range(2):
                add_blocks(down.at[i], r1.at[g, 1, i], 2)
            ring[g, name, "down3"] = links.start(down, r2.at[g, 1, hi], at(3))

    def ring_end(g):
        for name, (_, me, p, _, r2, total, at, other, r3) in (("a", stream_a), ("b", stream_b)):
            for part in ("up2", "down2", "up3", "down3"):
                ring[g, name, part].wait_recv()
            for i in range(4):
                total[g, i] = (p[g, me, i].astype(F32) + r2[g, 0, i].astype(F32) + r2[g, 1, i].astype(F32)).astype(BF)
            for d in (2, 1, 3):
                ring[g, name, d] = links.start(total.at[g, (other + d) % 4], r3.at[g, d - 1], at(d))

    def plane_copy(zz):
        away = (zz - z + 8) % 8
        slot = (away + 7) % 8
        return pltpu.make_async_remote_copy(
            src_ref=kz.at[zz],
            dst_ref=rkz.at[slot],
            send_sem=kz_send.at[zz],
            recv_sem=kz_recv.at[slot],
            device_id=dev(x, y, zz, c),
            device_id_type=MESH,
        )

    def ring_last(g):
        for name, (_, _, _, _, _, total, _, other, r3) in (("a", stream_a), ("b", stream_b)):
            for d in (1, 2, 3):
                ring[g, name, d].wait_recv()
            mine = total[g, other].astype(F32)
            for d in range(3):
                mine += r3[g, d].astype(F32)
            rows = pl.ds(0, 64) if name == "a" else pl.ds(64, 64)
            kz[pl.ds(2 * g, 2), rows, :] = mine.astype(BF)
        for zz in (2 * g, 2 * g + 1):

            @pl.when(z != zz)
            def _():
                plane_copy(zz).start()

    def spot(ref, zz, ll, cc):
        row = ll * 512 + cc * 256 + (zz % 2) * 128
        return ref.at[
            pl.ds(pl.multiple_of(row, 128), 128), pl.ds(pl.multiple_of((zz // 2) * 128, 128), 128)
        ]

    def gather_start(ref, total):
        place = spot(ref, z, l, c)
        place[...] = jnp.transpose(total).astype(BF)
        state = {"z": {}, "in": {}, "sib": {}}
        for d in (4, 3, 5, 2, 6, 1, 7):
            state["z"][d] = links.start(place, place, at_z(d))
        state["in"][0] = links.start(place, place, inner)
        state["sib"][0, 0] = links.start(place, place, sib)
        return state

    def gather_mid(ref, state):
        for d in (1, 7, 2, 6, 3, 5, 4):
            state["z"][d].wait_recv()
            place = spot(ref, (z + 8 - d) % 8, l, c)
            state["in"][d] = links.start(place, place, inner)
            state["sib"][d, 0] = links.start(place, place, sib)

    def gather_end(ref, state):
        for d in (0, 1, 7, 2, 6, 3, 5, 4):
            state["in"][d].wait_recv()
            place = spot(ref, (z + 8 - d) % 8, 1 - l, c)
            state["sib"][d, 1] = links.start(place, place, sib)

    top, low = pl.ds(0, 64), pl.ds(64, 64)
    v_block = z_at(0)
    v_copies = {}

    def v_first():
        for di in (0, 1):
            z_copies[di, 2, 1].wait_recv()
            z_copies[di, 3, 0].wait_recv()
        for xx in range(4):
            up = rz.at[0, 3, xx] if xx < 2 else rz.at[0, 2, xx]
            down = rz.at[1, 2, xx + 2] if xx < 2 else rz.at[1, 3, xx - 2]
            for yy in range(4):
                v_block[xx, yy] = (v_block[xx, yy].astype(F32) + up[yy].astype(F32) + down[yy].astype(F32)).astype(BF)
        for d in (2, 1, 3):
            v_copies["a", d] = links.start(v_block.at[(x + d) % 4, :, top], va1.at[d - 1], at_x(d))
            v_copies["b", d] = links.start(v_block.at[:, (y + d) % 4, low], vb1.at[d - 1], at_y(d))

    def v_wait():
        for d in (1, 2, 3):
            v_copies["a", d].wait_recv()
            v_copies["b", d].wait_recv()

    def v_second():
        v_wait()
        for i in range(4):
            total_a = v_block[x, i, top].astype(F32)
            total_b = v_block[i, y, low].astype(F32)
            for d in range(3):
                total_a += va1[d, i].astype(F32)
                total_b += vb1[d, i].astype(F32)
            va2[i] = total_a.astype(BF)
            vb2[i] = total_b.astype(BF)
        for d in (2, 1, 3):
            v_copies["a", d] = links.start(va2.at[(y + d) % 4], va3.at[d - 1], at_y(d))
            v_copies["b", d] = links.start(vb2.at[(x + d) % 4], vb3.at[d - 1], at_x(d))

    def v_third():
        v_wait()
        total_a, total_b = va2[y].astype(F32), vb2[x].astype(F32)
        for d in range(3):
            total_a += va3[d].astype(F32)
            total_b += vb3[d].astype(F32)
        return gather_start(out_v, jnp.concatenate([total_a, total_b], axis=0))

    backward(0)
    backward(1)
    grad_k(0)
    ring_start(0)
    backward(2)
    grad_k(1)
    ring_start(1)
    ring_pass(0)
    backward(3)
    grad_k(2)
    ring_start(2)
    ring_pass(1)
    grad_k(3)
    ring_start(3)
    z_step(3)
    ring_pass(2)
    ring_pass(3)
    ring_end(0)
    ring_end(1)
    ring_last(0)
    v_first()
    ring_end(2)
    ring_last(1)
    ring_end(3)
    ring_last(2)
    v_second()
    ring_last(3)
    gv = v_third()
    total_k = kz[z].astype(F32)
    for slot in range(7):
        pltpu.make_async_remote_copy(
            src_ref=kz.at[0], dst_ref=rkz.at[slot], send_sem=kz_send.at[0], recv_sem=kz_recv.at[slot],
            device_id=sib, device_id_type=MESH,
        ).wait_recv()
        total_k += rkz[slot].astype(F32)
    gk = gather_start(out_k, total_k)
    gather_mid(out_v, gv)
    gather_mid(out_k, gk)
    gather_end(out_v, gv)
    gather_end(out_k, gk)
    for state in (gv, gk):
        for copy in state["sib"].values():
            copy.wait_recv()
    for copy in links.all:
        copy.wait_send()
    for zz in range(8):

        @pl.when(z != zz)
        def _():
            plane_copy(zz).wait_send()


def widen(k_ref, v_ref, k_out, v_out):
    k_out[...] = k_ref[...].astype(F32)
    v_out[...] = v_ref[...].astype(F32)


def rotary_tables():
    half = HD // 2
    freqs = np.float32(ROPE_BASE) ** (-2.0 * np.arange(half, dtype=np.float32) / HD)
    angles = np.arange(LEN, dtype=np.float32)[:, None] * freqs.astype(np.float32)[None, :]
    cosine, sine = np.cos(angles), np.sin(angles)
    return (
        np.concatenate([cosine, cosine], axis=1).astype(np.float32),
        np.concatenate([sine, -sine], axis=1).astype(np.float32),
    )


def shards(hidden_in, queries, keys, d_attn, value_weight, pair_margin, pair_chosen):
    cosine, sine = rotary_tables()
    vmem = pl.BlockSpec(memory_space=pltpu.VMEM)
    anywhere = pl.BlockSpec(memory_space=pl.ANY)
    block = (128, 128)
    key_grad, value_grad = pl.pallas_call(
        kernel,
        name="projection_grads",
        out_shape=[jax.ShapeDtypeStruct((1024, 512), BF)] * 2,
        in_specs=[vmem] * 2 + [anywhere] * 7,
        out_specs=[vmem] * 2,
        scratch_shapes=[
            pltpu.VMEM((LEN, HD), F32),
            pltpu.VMEM((LEN, HD), F32),
            pltpu.VMEM((TOK, 4096), BF),
            pltpu.VMEM((TOK, 512), BF),
            pltpu.VMEM((TOK, 4096), BF),
            pltpu.VMEM((16, 2, TOK, 256), BF),
            pltpu.VMEM((16, 256, 512), BF),
            pltpu.VMEM((8, LEN, COLS), F32),
            pltpu.VMEM((8, COLS, HD), BF),
            pltpu.VMEM((8, COLS, HD), BF),
            pltpu.VMEM((2, TOK, 512), F32),
            pltpu.VMEM((TOK, 512), F32),
            pltpu.VMEM((TOK, 512), BF),
            pltpu.VMEM((2, TOK, 512), BF),
            pltpu.VMEM((4, 2, TOK, HD), BF),
            pltpu.VMEM((8, 4, 4) + block, BF),
            pltpu.VMEM((2, 4, 4, 4) + block, BF),
        ]
        + [
            pltpu.VMEM((3, 4, 64, 128), BF),
            pltpu.VMEM((4, 64, 128), BF),
            pltpu.VMEM((3, 64, 128), BF),
        ]
        * 2
        + [
            pltpu.VMEM((4, 4, 4, 2, 64, 128), BF),
            pltpu.VMEM((4, 2, 2, 2, 64, 128), BF),
            pltpu.VMEM((4, 2, 4, 2, 64, 128), BF),
            pltpu.VMEM((4, 4, 2, 64, 128), BF),
            pltpu.VMEM((4, 3, 2, 64, 128), BF),
        ]
        * 2
        + [
            pltpu.VMEM((8,) + block, BF),
            pltpu.VMEM((7,) + block, BF),
            pltpu.SemaphoreType.DMA((260,)),
            pltpu.SemaphoreType.DMA((260,)),
            pltpu.SemaphoreType.DMA((23,)),
            pltpu.SemaphoreType.DMA((8,)),
            pltpu.SemaphoreType.DMA((7,)),
        ],
        compiler_params=pltpu.CompilerParams(
            collective_id=0, has_side_effects=True, vmem_limit_bytes=58 * 2**20
        ),
    )(
        pair_margin.reshape(1, 1),
        pair_chosen.reshape(1, 1),
        jnp.asarray(cosine),
        jnp.asarray(sine),
        queries,
        keys,
        d_attn,
        hidden_in,
        value_weight,
    )
    part = pl.BlockSpec((512, 512), lambda i: (i, 0))
    return pl.pallas_call(
        widen,
        name="widen",
        grid=(2,),
        out_shape=[jax.ShapeDtypeStruct((1024, 512), F32)] * 2,
        in_specs=[part] * 2,
        out_specs=[part] * 2,
    )(key_grad, value_grad)


def solution(mesh):
    placed = (
        P(("rep", "shard"), None),
        P(("rep", "shard"), None),
        P(("rep", "shard"), None),
        P(("rep", "shard"), None),
        P("shard", None),
        P(("rep", "shard")),
        P(("rep", "shard")),
    )
    return jax.shard_map(
        shards,
        mesh=mesh,
        in_specs=placed,
        out_specs=(P("shard", None), P("shard", None)),
        check_vma=False,
    )
```

```python
import functools
import math

import jax
import jax.numpy as jnp
import numpy as np
from jax import lax
from jax.experimental import pallas as pl
from jax.experimental.pallas import tpu as pltpu
from jax.sharding import PartitionSpec as P

HD = 128
LEN = 96
TOK = 192
HEADS = 4
GROUP = 8
COLS = GROUP * LEN
BETA_SPIN = 0.1
ROPE_BASE = 500000.0
SCALE = 1.0 / math.sqrt(HD)
MESH = pl.DeviceIdType.MESH
BF = jnp.bfloat16
F32 = jnp.float32


class Links:
    def __init__(self, send, recv):
        self.send, self.recv, self.count, self.all = send, recv, 0, []

    def start(self, src, dst, device):
        copy = pltpu.make_async_remote_copy(
            src_ref=src,
            dst_ref=dst,
            send_sem=self.send.at[self.count],
            recv_sem=self.recv.at[self.count],
            device_id=device,
            device_id_type=MESH,
        )
        copy.start()
        self.count += 1
        self.all.append(copy)
        return copy


def add_blocks(dst, src, count):
    for i in range(count):
        dst[i] = (dst[i].astype(F32) + src[i].astype(F32)).astype(BF)


def kernel(
    margin, chosen, cos_hbm, sin_hbm, q_hbm, k_hbm, da_hbm, x_hbm, wv_hbm,
    out_k, out_v,
    cosine, sine, q, k, da,
    xc, wc, probs, sc, qc, acc, vr, vals, dvb, dkb,
    pv, rz, va1, va2, va3, vb1, vb2, vb3,
    pa, ra1, ra2, qa, ra3,
    pb, rb1, rb2, qb, rb3,
    kz, rkz, send, recv, local, kz_send, kz_recv,
):
    rep, shard = lax.axis_index("rep"), lax.axis_index("shard")
    z, l, c = rep // 4, (rep // 2) % 2, rep % 2
    h, y = shard // 4, shard % 4
    x = 2 * h + l

    def dev(xx, yy, zz, cc):
        return (zz * 4 + (xx % 2) * 2 + cc, (xx // 2) * 4 + yy)

    def at_x(d):
        return dev((x + d) % 4, y, z, c)

    def at_y(d):
        return dev(x, (y + d) % 4, z, c)

    def at_z(d):
        return dev(x, y, (z + d) % 8, c)

    sib = dev(x, y, z, 1 - c)
    outer = dev(3 - x, y, z, c)
    inner = dev(2 * h + 1 - l, y, z, c)

    peers = [sib] + [at_x(d) for d in (1, 2, 3)] + [at_y(d) for d in (1, 2, 3)] + [at_z(d) for d in range(1, 8)]
    barrier = pltpu.get_barrier_semaphore()
    for peer in peers:
        pl.semaphore_signal(barrier, inc=1, device_id=peer, device_id_type=MESH)

    kept = []

    def keep(src, dst):
        copy = pltpu.make_async_copy(src, dst, local.at[len(kept)])
        copy.start()
        kept.append(copy)

    def rows_of(quarter):
        return pl.ds(pl.multiple_of(quarter * 512 + c * 256, 256), 256)

    def columns_of(xx, yy, core):
        return pl.ds(pl.multiple_of((xx // 2) * 4096 + yy * 1024 + (xx % 2) * 512 + core * 256, 256), 256)

    for src, dst in ((q_hbm, q), (k_hbm, k), (da_hbm, da), (cos_hbm, cosine), (sin_hbm, sine)):
        keep(src, dst)
    for xx in range(4):
        for yy in range(4):
            keep(x_hbm.at[:, columns_of(xx, yy, c)], xc.at[xx * 4 + yy, c])
    for quarter in range(2):
        keep(wv_hbm.at[rows_of(quarter)], wc.at[(2 * h + quarter) * 4 + y])

    pl.semaphore_wait(barrier, len(peers))

    links = Links(send, recv)
    first = 1 - l
    w_outer = {0: links.start(wv_hbm.at[rows_of(first)], wc.at[(2 * h + first) * 4 + y], outer)}
    w_y = {}
    for quarter in (first, l):
        for d in (1, 3, 2):
            w_y[d, quarter is first] = links.start(
                wv_hbm.at[rows_of(quarter)], wc.at[(2 * h + quarter) * 4 + y], at_y(d)
            )
    xs = []
    for xx in range(4):
        for yy in range(4):
            xs.append(links.start(x_hbm.at[:, columns_of(xx, yy, 1 - c)], xc.at[xx * 4 + yy, c], sib))

    strength = BETA_SPIN / (1.0 + jnp.exp(BETA_SPIN * margin[...]))
    weight = strength * (2 * chosen[...] - 1).astype(F32)
    s_pos = lax.broadcasted_iota(jnp.int32, (LEN, COLS), 0)
    t_pos = lax.broadcasted_iota(jnp.int32, (LEN, COLS), 1) % LEN
    allowed = s_pos <= t_pos
    for copy in kept[:5]:
        copy.wait()

    def forward(g):
        for seq in range(2):
            unit = 2 * g + seq
            rows = pl.ds(seq * LEN, LEN)
            w = weight if seq == 0 else -weight
            for head in range(GROUP):
                cols = pl.ds((g * GROUP + head) * HD, HD)
                span = pl.ds(head * LEN, LEN)
                qc[unit, span, :] = q[rows, cols]
                sc[unit, span, :] = (da[rows, cols].astype(F32) * w).astype(BF)
            kcols = pl.ds(g * HD, HD)
            scores = lax.dot_general(
                k[rows, kcols], qc[unit], (((1,), (1,)), ((), ())), preferred_element_type=F32
            ) * SCALE
            scores = jnp.where(allowed, scores, -jnp.inf)
            top = jnp.max(scores, axis=0, keepdims=True)
            expo = jnp.exp(scores - top)
            p = expo / jnp.sum(expo, axis=0, keepdims=True)
            probs[unit] = p
            dv = jnp.dot(p.astype(BF), sc[unit], preferred_element_type=F32)
            dvb[c, rows, kcols] = dv.astype(BF)

    for g in range(HEADS):
        forward(g)
    dv_copy = links.start(dvb.at[c], dvb.at[c], sib)
    for copy in kept[5:]:
        copy.wait()
    for copy in xs:
        copy.wait_recv()
    dv_copy.wait_recv()

    dt = jnp.transpose(dvb[...].reshape(2 * TOK, 512).astype(F32)).astype(BF)

    def grad_v(xx, carry):
        for yy in range(4):
            out = jnp.dot(dt, xc[xx * 4 + yy].reshape(2 * TOK, 256), preferred_element_type=F32).astype(BF)
            for zz in range(8):
                cb, rh = zz // 2, zz % 2
                pv[zz, xx, yy] = out[cb * 128 : (cb + 1) * 128, rh * 128 : (rh + 1) * 128]
        return carry

    lax.fori_loop(0, 4, grad_v, 0)

    half_a, half_b = pl.ds(0, 2), pl.ds(2, 2)

    def z_at(d):
        return pv.at[(z + d + 8) % 8]

    z_copies = {}

    def z_add(dst, src):
        for i in range(2):
            add_blocks(dst.at[i], src.at[i], 4)

    def z_step(step):
        for di, sign in ((0, 1), (1, -1)):
            lead, other = (half_a, half_b) if sign == 1 else (half_b, half_a)
            far = z_at(sign * (4 - step)).at[lead]
            near = z_at(sign * (3 - step)).at[other]
            if step > 0:
                z_copies[di, step - 1, 0].wait_recv()
                z_add(far, rz.at[di, step - 1, half_a])
            z_copies[di, step, 0] = links.start(far, rz.at[di, step, half_a], at_z(sign + 8))
            if step < 3:
                if step > 0:
                    z_copies[di, step - 1, 1].wait_recv()
                    z_add(near, rz.at[di, step - 1, half_b])
                z_copies[di, step, 1] = links.start(near, rz.at[di, step, half_b], at_z(sign + 8))

    z_step(0)

    def product(tokens, indices):
        total = None
        for j in indices:
            left = xc[j].reshape(2 * TOK, 256) if tokens is None else xc[j, tokens]
            part = jnp.dot(left, wc[j], preferred_element_type=F32)
            total = part if total is None else total + part
        return total

    def pass_outer(d):
        w_y[d, True].wait_recv()
        block = wc.at[(2 * h + first) * 4 + (y + 4 - d) % 4]
        w_outer[d] = []
        parts = 4 if d == 2 else 2
        for part in range(parts):
            piece = block.at[pl.ds(part * (256 // parts), 256 // parts)]
            w_outer[d].append(links.start(piece, piece, outer))

    w_inner = []

    def pass_inner(d):
        block = wc.at[(2 * (1 - h) + l) * 4 + (y + 4 - d) % 4]
        copies = w_outer[d] if d else [w_outer[0]]
        for part, copy in enumerate(copies):
            copy.wait_recv()
            size = 256 // len(copies)
            piece = block.at[pl.ds(part * size, size)]
            w_inner.append(links.start(piece, piece, inner))

    pass_outer(1)
    pass_outer(3)
    pass_inner(0)
    acc[...] = product(None, [(2 * h + i) * 4 + y for i in range(2)]).reshape(2, TOK, 512)
    pass_outer(2)
    pass_inner(1)
    z_step(1)
    pass_inner(3)
    for d in (1, 3, 2):
        w_y[d, False].wait_recv()
    acc[...] += product(
        None, [(2 * h + i % 2) * 4 + (y + 1 + i // 2) % 4 for i in range(6)]
    ).reshape(2, TOK, 512)
    pass_inner(2)
    acc[...] += product(None, [(2 * (1 - h) + l) * 4 + i for i in range(4)]).reshape(2, TOK, 512)
    for copy in w_inner:
        copy.wait_recv()
    last = [(2 * (1 - h) + 1 - l) * 4 + i for i in range(4)]
    acc[1 - c] += product(1 - c, last)
    value_copy = links.start(acc.at[1 - c], vr, sib)
    acc[c] += product(c, last)
    z_step(2)
    value_copy.wait_recv()
    vals[...] = (acc[c] + vr[...]).astype(BF)

    dk_copies = {}

    def backward(g):
        kcols = pl.ds(g * HD, HD)
        for seq in range(2):
            unit = 2 * g + seq
            rows = pl.ds(seq * LEN, LEN)
            dp = lax.dot_general(
                vals[rows, kcols], sc[unit], (((1,), (1,)), ((), ())), preferred_element_type=F32
            )
            p = probs[unit]
            mean = jnp.sum(p * dp, axis=0, keepdims=True)
            ds = (p * (dp - mean) * SCALE).astype(BF)
            rot = jnp.dot(ds, qc[unit], preferred_element_type=F32)
            swapped = jnp.concatenate([rot[:, HD // 2 :], rot[:, : HD // 2]], axis=1)
            dkb[g, c, rows, :] = (rot * cosine[...] + swapped * sine[...]).astype(BF)
        dk_copies[g] = links.start(dkb.at[g, c], dkb.at[g, c], sib)

    def grad_k(g):
        dk_copies[g].wait_recv()
        dt = jnp.transpose(dkb[g].reshape(2 * TOK, HD).astype(F32)).astype(BF)
        for i in range(16):
            out = jnp.dot(dt, xc[i].reshape(2 * TOK, 256), preferred_element_type=F32).astype(BF)
            for rh in range(2):
                pa[g, i // 4, i % 4, rh] = out[:64, rh * 128 : (rh + 1) * 128]
                pb[g, i % 4, i // 4, rh] = out[64:, rh * 128 : (rh + 1) * 128]

    stream_a = (at_x, x, pa, ra1, ra2, qa, at_y, y, ra3)
    stream_b = (at_y, y, pb, rb1, rb2, qb, at_x, x, rb3)
    lo, hi = pl.ds(0, 2), pl.ds(2, 2)
    ring = {}

    def ring_start(g):
        for name, (at, me, p, r1, r2, _, _, _, _) in (("a", stream_a), ("b", stream_b)):
            far = p.at[g, (me + 2) % 4]
            ring[g, name, "up1"] = links.start(far.at[lo], r1.at[g, 0], at(1))
            ring[g, name, "down1"] = links.start(far.at[hi], r1.at[g, 1], at(3))
        for name, (at, me, p, r1, r2, _, _, _, _) in (("a", stream_a), ("b", stream_b)):
            up, down = p.at[g, (me + 1) % 4], p.at[g, (me + 3) % 4]
            ring[g, name, "up2"] = links.start(up.at[hi], r2.at[g, 0, hi], at(1))
            ring[g, name, "down2"] = links.start(down.at[lo], r2.at[g, 1, lo], at(3))

    def ring_pass(g):
        for name, (at, me, p, r1, r2, _, _, _, _) in (("a", stream_a), ("b", stream_b)):
            up, down = p.at[g, (me + 1) % 4].at[lo], p.at[g, (me + 3) % 4].at[hi]
            ring[g, name, "up1"].wait_recv()
            for i in range(2):
                add_blocks(up.at[i], r1.at[g, 0, i], 2)
            ring[g, name, "up3"] = links.start(up, r2.at[g, 0, lo], at(1))
            ring[g, name, "down1"].wait_recv()
            for i in range(2):
                add_blocks(down.at[i], r1.at[g, 1, i], 2)
            ring[g, name, "down3"] = links.start(down, r2.at[g, 1, hi], at(3))

    def ring_end(g):
        for name, (_, me, p, _, r2, total, at, other, r3) in (("a", stream_a), ("b", stream_b)):
            for part in ("up2", "down2", "up3", "down3"):
                ring[g, name, part].wait_recv()
            for i in range(4):
                total[g, i] = (p[g, me, i].astype(F32) + r2[g, 0, i].astype(F32) + r2[g, 1, i].astype(F32)).astype(BF)
            for d in (2, 1, 3):
                ring[g, name, d] = links.start(total.at[g, (other + d) % 4], r3.at[g, d - 1], at(d))

    def plane_copy(zz):
        away = (zz - z + 8) % 8
        slot = (away + 7) % 8
        return pltpu.make_async_remote_copy(
            src_ref=kz.at[zz],
            dst_ref=rkz.at[slot],
            send_sem=kz_send.at[zz],
            recv_sem=kz_recv.at[slot],
            device_id=dev(x, y, zz, c),
            device_id_type=MESH,
        )

    def ring_last(g):
        for name, (_, _, _, _, _, total, _, other, r3) in (("a", stream_a), ("b", stream_b)):
            for d in (1, 2, 3):
                ring[g, name, d].wait_recv()
            mine = total[g, other].astype(F32)
            for d in range(3):
                mine += r3[g, d].astype(F32)
            rows = pl.ds(0, 64) if name == "a" else pl.ds(64, 64)
            kz[pl.ds(2 * g, 2), rows, :] = mine.astype(BF)
        for zz in (2 * g, 2 * g + 1):

            @pl.when(z != zz)
            def _():
                plane_copy(zz).start()

    def spot(ref, zz, ll, cc):
        row = ll * 512 + cc * 256 + (zz % 2) * 128
        return ref.at[
            pl.ds(pl.multiple_of(row, 128), 128), pl.ds(pl.multiple_of((zz // 2) * 128, 128), 128)
        ]

    def gather_start(ref, total):
        place = spot(ref, z, l, c)
        place[...] = jnp.transpose(total).astype(BF)
        state = {"z": {}, "in": {}, "sib": {}}
        for d in (1, 7, 2, 6, 3, 5, 4):
            state["z"][d] = links.start(place, place, at_z(d))
        state["in"][0] = links.start(place, place, inner)
        state["sib"][0, 0] = links.start(place, place, sib)
        return state

    def gather_mid(ref, state):
        for d in (1, 7, 2, 6, 3, 5, 4):
            state["z"][d].wait_recv()
            place = spot(ref, (z + 8 - d) % 8, l, c)
            state["in"][d] = links.start(place, place, inner)
            state["sib"][d, 0] = links.start(place, place, sib)

    def gather_end(ref, state):
        for d in (0, 1, 7, 2, 6, 3, 5, 4):
            state["in"][d].wait_recv()
            place = spot(ref, (z + 8 - d) % 8, 1 - l, c)
            state["sib"][d, 1] = links.start(place, place, sib)

    top, low = pl.ds(0, 64), pl.ds(64, 64)
    v_block = z_at(0)
    v_copies = {}

    def v_first():
        for di in (0, 1):
            z_copies[di, 2, 1].wait_recv()
            z_copies[di, 3, 0].wait_recv()
        for xx in range(4):
            up = rz.at[0, 3, xx] if xx < 2 else rz.at[0, 2, xx]
            down = rz.at[1, 2, xx + 2] if xx < 2 else rz.at[1, 3, xx - 2]
            for yy in range(4):
                v_block[xx, yy] = (v_block[xx, yy].astype(F32) + up[yy].astype(F32) + down[yy].astype(F32)).astype(BF)
        for d in (2, 1, 3):
            v_copies["a", d] = links.start(v_block.at[(x + d) % 4, :, top], va1.at[d - 1], at_x(d))
            v_copies["b", d] = links.start(v_block.at[:, (y + d) % 4, low], vb1.at[d - 1], at_y(d))

    def v_wait():
        for d in (1, 2, 3):
            v_copies["a", d].wait_recv()
            v_copies["b", d].wait_recv()

    def v_second():
        v_wait()
        for i in range(4):
            total_a = v_block[x, i, top].astype(F32)
            total_b = v_block[i, y, low].astype(F32)
            for d in range(3):
                total_a += va1[d, i].astype(F32)
                total_b += vb1[d, i].astype(F32)
            va2[i] = total_a.astype(BF)
            vb2[i] = total_b.astype(BF)
        for d in (2, 1, 3):
            v_copies["a", d] = links.start(va2.at[(y + d) % 4], va3.at[d - 1], at_y(d))
            v_copies["b", d] = links.start(vb2.at[(x + d) % 4], vb3.at[d - 1], at_x(d))

    def v_third():
        v_wait()
        total_a, total_b = va2[y].astype(F32), vb2[x].astype(F32)
        for d in range(3):
            total_a += va3[d].astype(F32)
            total_b += vb3[d].astype(F32)
        return gather_start(out_v, jnp.concatenate([total_a, total_b], axis=0))

    backward(0)
    backward(1)
    grad_k(0)
    ring_start(0)
    backward(2)
    grad_k(1)
    ring_start(1)
    ring_pass(0)
    backward(3)
    grad_k(2)
    ring_start(2)
    ring_pass(1)
    grad_k(3)
    ring_start(3)
    ring_pass(2)
    z_step(3)
    ring_pass(3)
    ring_end(0)
    ring_end(1)
    ring_last(0)
    ring_end(2)
    ring_last(1)
    ring_end(3)
    v_first()
    ring_last(2)
    ring_last(3)
    v_second()
    gv = v_third()
    total_k = kz[z].astype(F32)
    for slot in range(7):
        pltpu.make_async_remote_copy(
            src_ref=kz.at[0], dst_ref=rkz.at[slot], send_sem=kz_send.at[0], recv_sem=kz_recv.at[slot],
            device_id=sib, device_id_type=MESH,
        ).wait_recv()
        total_k += rkz[slot].astype(F32)
    gk = gather_start(out_k, total_k)
    gather_mid(out_v, gv)
    gather_mid(out_k, gk)
    gather_end(out_v, gv)
    gather_end(out_k, gk)
    for state in (gv, gk):
        for copy in state["sib"].values():
            copy.wait_recv()
    for copy in links.all:
        copy.wait_send()
    for zz in range(8):

        @pl.when(z != zz)
        def _():
            plane_copy(zz).wait_send()


def widen(k_ref, v_ref, k_out, v_out, k_wide, v_wide, sems):
    copies = []
    for part in range(2):
        rows = pl.ds(part * 512, 512)
        for i, (ref, wide, out) in enumerate(((k_ref, k_wide, k_out), (v_ref, v_wide, v_out))):
            wide[rows, :] = ref[rows, :].astype(F32)
            copy = pltpu.make_async_copy(wide.at[rows], out.at[rows], sems.at[part, i])
            copy.start()
            copies.append(copy)
    for copy in copies:
        copy.wait()


def rotary_tables():
    half = HD // 2
    freqs = np.float32(ROPE_BASE) ** (-2.0 * np.arange(half, dtype=np.float32) / HD)
    angles = np.arange(LEN, dtype=np.float32)[:, None] * freqs.astype(np.float32)[None, :]
    cosine, sine = np.cos(angles), np.sin(angles)
    return (
        np.concatenate([cosine, cosine], axis=1).astype(np.float32),
        np.concatenate([sine, -sine], axis=1).astype(np.float32),
    )


def shards(hidden_in, queries, keys, d_attn, value_weight, pair_margin, pair_chosen):
    cosine, sine = rotary_tables()
    vmem = pl.BlockSpec(memory_space=pltpu.VMEM)
    anywhere = pl.BlockSpec(memory_space=pltpu.HBM)
    block = (128, 128)
    key_grad, value_grad = pl.pallas_call(
        kernel,
        name="projection_grads",
        out_shape=[pltpu.VMEM((1024, 512), BF)] * 2,
        in_specs=[vmem] * 2 + [anywhere] * 7,
        out_specs=[vmem] * 2,
        scratch_shapes=[
            pltpu.VMEM((LEN, HD), F32),
            pltpu.VMEM((LEN, HD), F32),
            pltpu.VMEM((TOK, 4096), BF),
            pltpu.VMEM((TOK, 512), BF),
            pltpu.VMEM((TOK, 4096), BF),
            pltpu.VMEM((16, 2, TOK, 256), BF),
            pltpu.VMEM((16, 256, 512), BF),
            pltpu.VMEM((8, LEN, COLS), F32),
            pltpu.VMEM((8, COLS, HD), BF),
            pltpu.VMEM((8, COLS, HD), BF),
            pltpu.VMEM((2, TOK, 512), F32),
            pltpu.VMEM((TOK, 512), F32),
            pltpu.VMEM((TOK, 512), BF),
            pltpu.VMEM((2, TOK, 512), BF),
            pltpu.VMEM((4, 2, TOK, HD), BF),
            pltpu.VMEM((8, 4, 4) + block, BF),
            pltpu.VMEM((2, 4, 4, 4) + block, BF),
        ]
        + [
            pltpu.VMEM((3, 4, 64, 128), BF),
            pltpu.VMEM((4, 64, 128), BF),
            pltpu.VMEM((3, 64, 128), BF),
        ]
        * 2
        + [
            pltpu.VMEM((4, 4, 4, 2, 64, 128), BF),
            pltpu.VMEM((4, 2, 2, 2, 64, 128), BF),
            pltpu.VMEM((4, 2, 4, 2, 64, 128), BF),
            pltpu.VMEM((4, 4, 2, 64, 128), BF),
            pltpu.VMEM((4, 3, 2, 64, 128), BF),
        ]
        * 2
        + [
            pltpu.VMEM((8,) + block, BF),
            pltpu.VMEM((7,) + block, BF),
            pltpu.SemaphoreType.DMA((260,)),
            pltpu.SemaphoreType.DMA((260,)),
            pltpu.SemaphoreType.DMA((23,)),
            pltpu.SemaphoreType.DMA((8,)),
            pltpu.SemaphoreType.DMA((7,)),
        ],
        compiler_params=pltpu.CompilerParams(
            collective_id=0, has_side_effects=True, vmem_limit_bytes=56 * 2**20
        ),
    )(
        pair_margin.reshape(1, 1),
        pair_chosen.reshape(1, 1),
        jnp.asarray(cosine),
        jnp.asarray(sine),
        queries,
        keys,
        d_attn,
        hidden_in,
        value_weight,
    )
    key_grad = pltpu.with_memory_space_constraint(key_grad, pltpu.VMEM)
    value_grad = pltpu.with_memory_space_constraint(value_grad, pltpu.VMEM)
    return pl.pallas_call(
        widen,
        name="widen",
        out_shape=[jax.ShapeDtypeStruct((1024, 512), F32)] * 2,
        in_specs=[vmem] * 2,
        out_specs=[anywhere] * 2,
        scratch_shapes=[pltpu.VMEM((1024, 512), F32)] * 2 + [pltpu.SemaphoreType.DMA((2, 2))],
        compiler_params=pltpu.CompilerParams(vmem_limit_bytes=40 * 2**20),
    )(key_grad, value_grad)


def solution(mesh):
    placed = (
        P(("rep", "shard"), None),
        P(("rep", "shard"), None),
        P(("rep", "shard"), None),
        P(("rep", "shard"), None),
        P("shard", None),
        P(("rep", "shard")),
        P(("rep", "shard")),
    )
    return jax.shard_map(
        shards,
        mesh=mesh,
        in_specs=placed,
        out_specs=(P("shard", None), P("shard", None)),
        check_vma=False,
    )
```

```python
import functools
import math

import jax
import jax.numpy as jnp
import numpy as np
from jax import lax
from jax.experimental import pallas as pl
from jax.experimental.pallas import tpu as pltpu
from jax.sharding import PartitionSpec as P

HD = 128
LEN = 96
TOK = 192
HEADS = 4
GROUP = 8
COLS = GROUP * LEN
BETA_SPIN = 0.1
ROPE_BASE = 500000.0
SCALE = 1.0 / math.sqrt(HD)
MESH = pl.DeviceIdType.MESH
BF = jnp.bfloat16
F32 = jnp.float32


class Links:
    def __init__(self, send, recv):
        self.send, self.recv, self.count, self.all = send, recv, 0, []

    def start(self, src, dst, device):
        copy = pltpu.make_async_remote_copy(
            src_ref=src,
            dst_ref=dst,
            send_sem=self.send.at[self.count],
            recv_sem=self.recv.at[self.count],
            device_id=device,
            device_id_type=MESH,
        )
        copy.start()
        self.count += 1
        self.all.append(copy)
        return copy


def add_blocks(dst, src, count):
    for i in range(count):
        dst[i] = (dst[i].astype(F32) + src[i].astype(F32)).astype(BF)


def kernel(
    margin, chosen, cos_hbm, sin_hbm, q_hbm, k_hbm, da_hbm, x_hbm, wv_hbm,
    out_k, out_v,
    cosine, sine, q, k, da,
    xc, wc, probs, sc, qc, acc, vr, vals, dvb, dkb,
    pv, rz, va1, va2, va3, vb1, vb2, vb3,
    pa, ra1, ra2, qa, ra3,
    pb, rb1, rb2, qb, rb3,
    kz, rkz, send, recv, local, kz_send, kz_recv,
):
    rep, shard = lax.axis_index("rep"), lax.axis_index("shard")
    z, l, c = rep // 4, (rep // 2) % 2, rep % 2
    h, y = shard // 4, shard % 4
    x = 2 * h + l

    def dev(xx, yy, zz, cc):
        return (zz * 4 + (xx % 2) * 2 + cc, (xx // 2) * 4 + yy)

    def at_x(d):
        return dev((x + d) % 4, y, z, c)

    def at_y(d):
        return dev(x, (y + d) % 4, z, c)

    def at_z(d):
        return dev(x, y, (z + d) % 8, c)

    sib = dev(x, y, z, 1 - c)
    outer = dev(3 - x, y, z, c)
    inner = dev(2 * h + 1 - l, y, z, c)

    peers = [sib] + [at_x(d) for d in (1, 2, 3)] + [at_y(d) for d in (1, 2, 3)] + [at_z(d) for d in range(1, 8)]
    barrier = pltpu.get_barrier_semaphore()
    for peer in peers:
        pl.semaphore_signal(barrier, inc=1, device_id=peer, device_id_type=MESH)

    kept = []

    def keep(src, dst):
        copy = pltpu.make_async_copy(src, dst, local.at[len(kept)])
        copy.start()
        kept.append(copy)

    def rows_of(quarter):
        return pl.ds(pl.multiple_of(quarter * 512 + c * 256, 256), 256)

    def columns_of(xx, yy, core):
        return pl.ds(pl.multiple_of((xx // 2) * 4096 + yy * 1024 + (xx % 2) * 512 + core * 256, 256), 256)

    for src, dst in ((q_hbm, q), (k_hbm, k), (da_hbm, da), (cos_hbm, cosine), (sin_hbm, sine)):
        keep(src, dst)
    for xx in range(4):
        for yy in range(4):
            keep(x_hbm.at[:, columns_of(xx, yy, c)], xc.at[xx * 4 + yy, c])
    for quarter in range(2):
        keep(wv_hbm.at[rows_of(quarter)], wc.at[(2 * h + quarter) * 4 + y])

    pl.semaphore_wait(barrier, len(peers))

    links = Links(send, recv)
    first = 1 - l
    w_outer = {0: links.start(wv_hbm.at[rows_of(first)], wc.at[(2 * h + first) * 4 + y], outer)}
    w_y = {}
    for quarter in (first, l):
        for d in (1, 3, 2):
            w_y[d, quarter is first] = links.start(
                wv_hbm.at[rows_of(quarter)], wc.at[(2 * h + quarter) * 4 + y], at_y(d)
            )
    xs = []
    for xx in range(4):
        for yy in range(4):
            xs.append(links.start(x_hbm.at[:, columns_of(xx, yy, 1 - c)], xc.at[xx * 4 + yy, c], sib))

    strength = BETA_SPIN / (1.0 + jnp.exp(BETA_SPIN * margin[...]))
    weight = strength * (2 * chosen[...] - 1).astype(F32)
    s_pos = lax.broadcasted_iota(jnp.int32, (LEN, COLS), 0)
    t_pos = lax.broadcasted_iota(jnp.int32, (LEN, COLS), 1) % LEN
    allowed = s_pos <= t_pos
    for copy in kept[:5]:
        copy.wait()

    def forward(g):
        for seq in range(2):
            unit = 2 * g + seq
            rows = pl.ds(seq * LEN, LEN)
            w = weight if seq == 0 else -weight
            for head in range(GROUP):
                cols = pl.ds((g * GROUP + head) * HD, HD)
                span = pl.ds(head * LEN, LEN)
                qc[unit, span, :] = q[rows, cols]
                sc[unit, span, :] = (da[rows, cols].astype(F32) * w).astype(BF)
            kcols = pl.ds(g * HD, HD)
            scores = lax.dot_general(
                k[rows, kcols], qc[unit], (((1,), (1,)), ((), ())), preferred_element_type=F32
            ) * SCALE
            scores = jnp.where(allowed, scores, -jnp.inf)
            top = jnp.max(scores, axis=0, keepdims=True)
            expo = jnp.exp(scores - top)
            p = expo / jnp.sum(expo, axis=0, keepdims=True)
            probs[unit] = p
            dv = jnp.dot(p.astype(BF), sc[unit], preferred_element_type=F32)
            dvb[c, rows, kcols] = dv.astype(BF)

    for g in range(HEADS):
        forward(g)
    dv_copy = links.start(dvb.at[c], dvb.at[c], sib)
    for copy in kept[5:]:
        copy.wait()
    for copy in xs:
        copy.wait_recv()
    dv_copy.wait_recv()

    dt = jnp.transpose(dvb[...].reshape(2 * TOK, 512).astype(F32)).astype(BF)

    def grad_v(xx, carry):
        for yy in range(4):
            out = jnp.dot(dt, xc[xx * 4 + yy].reshape(2 * TOK, 256), preferred_element_type=F32).astype(BF)
            for zz in range(8):
                cb, rh = zz // 2, zz % 2
                pv[zz, xx, yy] = out[cb * 128 : (cb + 1) * 128, rh * 128 : (rh + 1) * 128]
        return carry

    half_a, half_b = pl.ds(0, 2), pl.ds(2, 2)

    def z_at(d):
        return pv.at[(z + d + 8) % 8]

    z_copies = {}

    def z_add(dst, src):
        for i in range(2):
            add_blocks(dst.at[i], src.at[i], 4)

    def z_step(step):
        for di, sign in ((0, 1), (1, -1)):
            lead, other = (half_a, half_b) if sign == 1 else (half_b, half_a)
            far = z_at(sign * (4 - step)).at[lead]
            near = z_at(sign * (3 - step)).at[other]
            if step > 0:
                z_copies[di, step - 1, 0].wait_recv()
                z_add(far, rz.at[di, step - 1, half_a])
            z_copies[di, step, 0] = links.start(far, rz.at[di, step, half_a], at_z(sign + 8))
            if step < 3:
                if step > 0:
                    z_copies[di, step - 1, 1].wait_recv()
                    z_add(near, rz.at[di, step - 1, half_b])
                z_copies[di, step, 1] = links.start(near, rz.at[di, step, half_b], at_z(sign + 8))

    lax.fori_loop(0, 2, grad_v, 0)
    z_copies[0, 0, 0] = links.start(z_at(4).at[half_a], rz.at[0, 0, half_a], at_z(9))
    z_copies[1, 0, 1] = links.start(z_at(-3).at[half_a], rz.at[1, 0, half_b], at_z(7))
    lax.fori_loop(2, 4, grad_v, 0)
    z_copies[1, 0, 0] = links.start(z_at(-4).at[half_b], rz.at[1, 0, half_a], at_z(7))
    z_copies[0, 0, 1] = links.start(z_at(3).at[half_b], rz.at[0, 0, half_b], at_z(9))

    def product(tokens, indices):
        total = None
        for j in indices:
            left = xc[j].reshape(2 * TOK, 256) if tokens is None else xc[j, tokens]
            part = jnp.dot(left, wc[j], preferred_element_type=F32)
            total = part if total is None else total + part
        return total

    def pass_outer(d):
        w_y[d, True].wait_recv()
        block = wc.at[(2 * h + first) * 4 + (y + 4 - d) % 4]
        w_outer[d] = []
        parts = 4 if d == 2 else 2
        for part in range(parts):
            piece = block.at[pl.ds(part * (256 // parts), 256 // parts)]
            w_outer[d].append(links.start(piece, piece, outer))

    w_inner = []

    def pass_inner(d):
        block = wc.at[(2 * (1 - h) + l) * 4 + (y + 4 - d) % 4]
        copies = w_outer[d] if d else [w_outer[0]]
        for part, copy in enumerate(copies):
            copy.wait_recv()
            size = 256 // len(copies)
            piece = block.at[pl.ds(part * size, size)]
            w_inner.append(links.start(piece, piece, inner))

    pass_outer(1)
    pass_outer(3)
    pass_inner(0)
    acc[...] = product(None, [(2 * h + i) * 4 + y for i in range(2)]).reshape(2, TOK, 512)
    pass_outer(2)
    pass_inner(1)
    z_step(1)
    pass_inner(3)
    for d in (1, 3, 2):
        w_y[d, False].wait_recv()
    acc[...] += product(
        None, [(2 * h + i % 2) * 4 + (y + 1 + i // 2) % 4 for i in range(6)]
    ).reshape(2, TOK, 512)
    pass_inner(2)
    acc[...] += product(None, [(2 * (1 - h) + l) * 4 + i for i in range(4)]).reshape(2, TOK, 512)
    for copy in w_inner:
        copy.wait_recv()
    last = [(2 * (1 - h) + 1 - l) * 4 + i for i in range(4)]
    acc[1 - c] += product(1 - c, last)
    value_copy = links.start(acc.at[1 - c], vr, sib)
    acc[c] += product(c, last)
    z_step(2)
    value_copy.wait_recv()
    vals[...] = (acc[c] + vr[...]).astype(BF)

    dk_copies = {}

    def backward(g):
        kcols = pl.ds(g * HD, HD)
        for seq in range(2):
            unit = 2 * g + seq
            rows = pl.ds(seq * LEN, LEN)
            dp = lax.dot_general(
                vals[rows, kcols], sc[unit], (((1,), (1,)), ((), ())), preferred_element_type=F32
            )
            p = probs[unit]
            mean = jnp.sum(p * dp, axis=0, keepdims=True)
            ds = (p * (dp - mean) * SCALE).astype(BF)
            rot = jnp.dot(ds, qc[unit], preferred_element_type=F32)
            swapped = jnp.concatenate([rot[:, HD // 2 :], rot[:, : HD // 2]], axis=1)
            dkb[g, c, rows, :] = (rot * cosine[...] + swapped * sine[...]).astype(BF)
        dk_copies[g] = links.start(dkb.at[g, c], dkb.at[g, c], sib)

    def grad_k(g):
        dk_copies[g].wait_recv()
        dt = jnp.transpose(dkb[g].reshape(2 * TOK, HD).astype(F32)).astype(BF)
        for i in range(16):
            out = jnp.dot(dt, xc[i].reshape(2 * TOK, 256), preferred_element_type=F32).astype(BF)
            for rh in range(2):
                pa[g, i // 4, i % 4, rh] = out[:64, rh * 128 : (rh + 1) * 128]
                pb[g, i % 4, i // 4, rh] = out[64:, rh * 128 : (rh + 1) * 128]

    stream_a = (at_x, x, pa, ra1, ra2, qa, at_y, y, ra3)
    stream_b = (at_y, y, pb, rb1, rb2, qb, at_x, x, rb3)
    lo, hi = pl.ds(0, 2), pl.ds(2, 2)
    ring = {}

    def ring_start(g):
        for name, (at, me, p, r1, r2, _, _, _, _) in (("a", stream_a), ("b", stream_b)):
            far = p.at[g, (me + 2) % 4]
            ring[g, name, "up1"] = links.start(far.at[lo], r1.at[g, 0], at(1))
            ring[g, name, "down1"] = links.start(far.at[hi], r1.at[g, 1], at(3))
        for name, (at, me, p, r1, r2, _, _, _, _) in (("a", stream_a), ("b", stream_b)):
            up, down = p.at[g, (me + 1) % 4], p.at[g, (me + 3) % 4]
            ring[g, name, "up2"] = links.start(up.at[hi], r2.at[g, 0, hi], at(1))
            ring[g, name, "down2"] = links.start(down.at[lo], r2.at[g, 1, lo], at(3))

    def ring_pass(g):
        for name, (at, me, p, r1, r2, _, _, _, _) in (("a", stream_a), ("b", stream_b)):
            up, down = p.at[g, (me + 1) % 4].at[lo], p.at[g, (me + 3) % 4].at[hi]
            ring[g, name, "up1"].wait_recv()
            for i in range(2):
                add_blocks(up.at[i], r1.at[g, 0, i], 2)
            ring[g, name, "up3"] = links.start(up, r2.at[g, 0, lo], at(1))
            ring[g, name, "down1"].wait_recv()
            for i in range(2):
                add_blocks(down.at[i], r1.at[g, 1, i], 2)
            ring[g, name, "down3"] = links.start(down, r2.at[g, 1, hi], at(3))

    def ring_end(g):
        for name, (_, me, p, _, r2, total, at, other, r3) in (("a", stream_a), ("b", stream_b)):
            for part in ("up2", "down2", "up3", "down3"):
                ring[g, name, part].wait_recv()
            for i in range(4):
                total[g, i] = (p[g, me, i].astype(F32) + r2[g, 0, i].astype(F32) + r2[g, 1, i].astype(F32)).astype(BF)
            for d in (2, 1, 3):
                ring[g, name, d] = links.start(total.at[g, (other + d) % 4], r3.at[g, d - 1], at(d))

    def plane_copy(zz):
        away = (zz - z + 8) % 8
        slot = (away + 7) % 8
        return pltpu.make_async_remote_copy(
            src_ref=kz.at[zz],
            dst_ref=rkz.at[slot],
            send_sem=kz_send.at[zz],
            recv_sem=kz_recv.at[slot],
            device_id=dev(x, y, zz, c),
            device_id_type=MESH,
        )

    def ring_last(g):
        for name, (_, _, _, _, _, total, _, other, r3) in (("a", stream_a), ("b", stream_b)):
            for d in (1, 2, 3):
                ring[g, name, d].wait_recv()
            mine = total[g, other].astype(F32)
            for d in range(3):
                mine += r3[g, d].astype(F32)
            rows = pl.ds(0, 64) if name == "a" else pl.ds(64, 64)
            kz[pl.ds(2 * g, 2), rows, :] = mine.astype(BF)
        for zz in (2 * g, 2 * g + 1):

            @pl.when(z != zz)
            def _():
                plane_copy(zz).start()

    def spot(ref, zz, ll, cc):
        row = ll * 512 + cc * 256 + (zz % 2) * 128
        return ref.at[
            pl.ds(pl.multiple_of(row, 128), 128), pl.ds(pl.multiple_of((zz // 2) * 128, 128), 128)
        ]

    def gather_start(ref, total):
        place = spot(ref, z, l, c)
        place[...] = jnp.transpose(total).astype(BF)
        state = {"z": {}, "in": {}, "sib": {}}
        for d in (1, 7, 2, 6, 3, 5, 4):
            state["z"][d] = links.start(place, place, at_z(d))
        state["in"][0] = links.start(place, place, inner)
        state["sib"][0, 0] = links.start(place, place, sib)
        return state

    def gather_mid(ref, state):
        for d in (1, 7, 2, 6, 3, 5, 4):
            state["z"][d].wait_recv()
            place = spot(ref, (z + 8 - d) % 8, l, c)
            state["in"][d] = links.start(place, place, inner)
            state["sib"][d, 0] = links.start(place, place, sib)

    def gather_end(ref, state):
        for d in (0, 1, 7, 2, 6, 3, 5, 4):
            state["in"][d].wait_recv()
            place = spot(ref, (z + 8 - d) % 8, 1 - l, c)
            state["sib"][d, 1] = links.start(place, place, sib)

    top, low = pl.ds(0, 64), pl.ds(64, 64)
    v_block = z_at(0)
    v_copies = {}

    def v_first():
        for di in (0, 1):
            z_copies[di, 2, 1].wait_recv()
            z_copies[di, 3, 0].wait_recv()
        for xx in range(4):
            up = rz.at[0, 3, xx] if xx < 2 else rz.at[0, 2, xx]
            down = rz.at[1, 2, xx + 2] if xx < 2 else rz.at[1, 3, xx - 2]
            for yy in range(4):
                v_block[xx, yy] = (v_block[xx, yy].astype(F32) + up[yy].astype(F32) + down[yy].astype(F32)).astype(BF)
        for d in (2, 1, 3):
            v_copies["a", d] = links.start(v_block.at[(x + d) % 4, :, top], va1.at[d - 1], at_x(d))
            v_copies["b", d] = links.start(v_block.at[:, (y + d) % 4, low], vb1.at[d - 1], at_y(d))

    def v_wait():
        for d in (1, 2, 3):
            v_copies["a", d].wait_recv()
            v_copies["b", d].wait_recv()

    def v_second():
        v_wait()
        for i in range(4):
            total_a = v_block[x, i, top].astype(F32)
            total_b = v_block[i, y, low].astype(F32)
            for d in range(3):
                total_a += va1[d, i].astype(F32)
                total_b += vb1[d, i].astype(F32)
            va2[i] = total_a.astype(BF)
            vb2[i] = total_b.astype(BF)
        for d in (2, 1, 3):
            v_copies["a", d] = links.start(va2.at[(y + d) % 4], va3.at[d - 1], at_y(d))
            v_copies["b", d] = links.start(vb2.at[(x + d) % 4], vb3.at[d - 1], at_x(d))

    def v_third():
        v_wait()
        total_a, total_b = va2[y].astype(F32), vb2[x].astype(F32)
        for d in range(3):
            total_a += va3[d].astype(F32)
            total_b += vb3[d].astype(F32)
        return gather_start(out_v, jnp.concatenate([total_a, total_b], axis=0))

    backward(0)
    backward(1)
    grad_k(0)
    ring_start(0)
    backward(2)
    grad_k(1)
    ring_start(1)
    ring_pass(0)
    backward(3)
    grad_k(2)
    ring_start(2)
    ring_pass(1)
    grad_k(3)
    ring_start(3)
    ring_pass(2)
    z_step(3)
    ring_pass(3)
    ring_end(0)
    ring_end(1)
    ring_last(0)
    ring_end(2)
    ring_last(1)
    ring_end(3)
    v_first()
    ring_last(2)
    ring_last(3)
    v_second()
    gv = v_third()
    total_k = kz[z].astype(F32)
    for slot in range(7):
        pltpu.make_async_remote_copy(
            src_ref=kz.at[0], dst_ref=rkz.at[slot], send_sem=kz_send.at[0], recv_sem=kz_recv.at[slot],
            device_id=sib, device_id_type=MESH,
        ).wait_recv()
        total_k += rkz[slot].astype(F32)
    gk = gather_start(out_k, total_k)
    gather_mid(out_v, gv)
    gather_mid(out_k, gk)
    gather_end(out_v, gv)
    gather_end(out_k, gk)
    for state in (gv, gk):
        for copy in state["sib"].values():
            copy.wait_recv()
    for copy in links.all:
        copy.wait_send()
    for zz in range(8):

        @pl.when(z != zz)
        def _():
            plane_copy(zz).wait_send()


def widen(k_ref, v_ref, k_out, v_out, k_wide, v_wide, sems):
    copies = []
    for part in range(2):
        rows = pl.ds(part * 512, 512)
        for i, (ref, wide, out) in enumerate(((k_ref, k_wide, k_out), (v_ref, v_wide, v_out))):
            wide[rows, :] = ref[rows, :].astype(F32)
            copy = pltpu.make_async_copy(wide.at[rows], out.at[rows], sems.at[part, i])
            copy.start()
            copies.append(copy)
    for copy in copies:
        copy.wait()


def rotary_tables():
    half = HD // 2
    freqs = np.float32(ROPE_BASE) ** (-2.0 * np.arange(half, dtype=np.float32) / HD)
    angles = np.arange(LEN, dtype=np.float32)[:, None] * freqs.astype(np.float32)[None, :]
    cosine, sine = np.cos(angles), np.sin(angles)
    return (
        np.concatenate([cosine, cosine], axis=1).astype(np.float32),
        np.concatenate([sine, -sine], axis=1).astype(np.float32),
    )


def shards(hidden_in, queries, keys, d_attn, value_weight, pair_margin, pair_chosen):
    cosine, sine = rotary_tables()
    vmem = pl.BlockSpec(memory_space=pltpu.VMEM)
    anywhere = pl.BlockSpec(memory_space=pltpu.HBM)
    block = (128, 128)
    key_grad, value_grad = pl.pallas_call(
        kernel,
        name="projection_grads",
        out_shape=[pltpu.VMEM((1024, 512), BF)] * 2,
        in_specs=[vmem] * 2 + [anywhere] * 7,
        out_specs=[vmem] * 2,
        scratch_shapes=[
            pltpu.VMEM((LEN, HD), F32),
            pltpu.VMEM((LEN, HD), F32),
            pltpu.VMEM((TOK, 4096), BF),
            pltpu.VMEM((TOK, 512), BF),
            pltpu.VMEM((TOK, 4096), BF),
            pltpu.VMEM((16, 2, TOK, 256), BF),
            pltpu.VMEM((16, 256, 512), BF),
            pltpu.VMEM((8, LEN, COLS), F32),
            pltpu.VMEM((8, COLS, HD), BF),
            pltpu.VMEM((8, COLS, HD), BF),
            pltpu.VMEM((2, TOK, 512), F32),
            pltpu.VMEM((TOK, 512), F32),
            pltpu.VMEM((TOK, 512), BF),
            pltpu.VMEM((2, TOK, 512), BF),
            pltpu.VMEM((4, 2, TOK, HD), BF),
            pltpu.VMEM((8, 4, 4) + block, BF),
            pltpu.VMEM((2, 4, 4, 4) + block, BF),
        ]
        + [
            pltpu.VMEM((3, 4, 64, 128), BF),
            pltpu.VMEM((4, 64, 128), BF),
            pltpu.VMEM((3, 64, 128), BF),
        ]
        * 2
        + [
            pltpu.VMEM((4, 4, 4, 2, 64, 128), BF),
            pltpu.VMEM((4, 2, 2, 2, 64, 128), BF),
            pltpu.VMEM((4, 2, 4, 2, 64, 128), BF),
            pltpu.VMEM((4, 4, 2, 64, 128), BF),
            pltpu.VMEM((4, 3, 2, 64, 128), BF),
        ]
        * 2
        + [
            pltpu.VMEM((8,) + block, BF),
            pltpu.VMEM((7,) + block, BF),
            pltpu.SemaphoreType.DMA((260,)),
            pltpu.SemaphoreType.DMA((260,)),
            pltpu.SemaphoreType.DMA((23,)),
            pltpu.SemaphoreType.DMA((8,)),
            pltpu.SemaphoreType.DMA((7,)),
        ],
        compiler_params=pltpu.CompilerParams(
            collective_id=0, has_side_effects=True, vmem_limit_bytes=56 * 2**20
        ),
    )(
        pair_margin.reshape(1, 1),
        pair_chosen.reshape(1, 1),
        jnp.asarray(cosine),
        jnp.asarray(sine),
        queries,
        keys,
        d_attn,
        hidden_in,
        value_weight,
    )
    key_grad = pltpu.with_memory_space_constraint(key_grad, pltpu.VMEM)
    value_grad = pltpu.with_memory_space_constraint(value_grad, pltpu.VMEM)
    return pl.pallas_call(
        widen,
        name="widen",
        out_shape=[jax.ShapeDtypeStruct((1024, 512), F32)] * 2,
        in_specs=[vmem] * 2,
        out_specs=[anywhere] * 2,
        scratch_shapes=[pltpu.VMEM((1024, 512), F32)] * 2 + [pltpu.SemaphoreType.DMA((2, 2))],
        compiler_params=pltpu.CompilerParams(vmem_limit_bytes=40 * 2**20),
    )(key_grad, value_grad)


def solution(mesh):
    placed = (
        P(("rep", "shard"), None),
        P(("rep", "shard"), None),
        P(("rep", "shard"), None),
        P(("rep", "shard"), None),
        P("shard", None),
        P(("rep", "shard")),
        P(("rep", "shard")),
    )
    return jax.shard_map(
        shards,
        mesh=mesh,
        in_specs=placed,
        out_specs=(P("shard", None), P("shard", None)),
        check_vma=False,
    )
```
